32 devices in a mesh: phase: 2 (over core), space: 16 (over z, y, x).
Axes of the slice: x: 2, y: 2, z: 4, core: 2. Of those that a mesh axis runs over, the one named last changes fastest.
Arguments:
- features: bfloat16 [2, 8192, 256], P(None, 'space'), may hold values from -45 to 45
- weights: bfloat16 [2, 27, 256, 256], P('phase'), may hold values from -0.078125 to 0.078125
- conv_bias: float32 [2, 256], replicated, may hold values from -4 to 4
- rulebook: int32 [8192, 27], P('space'), may hold values from 0 to 576, as said below
- border: int32 [16, 64], P('space'), may hold values from 0 to 511, as said below
- pull_slots: int32 [16, 16, 4], P('space'), may hold values from 0 to 63
Outputs:
- section_outputs: bfloat16 [2, 2, 8192, 256], P('phase', None, 'space')
The draws below stay inside these ranges and needn't reach their ends.
Inputs may be any that keep to these rules, and one draw needn't show every extreme that they name: `rulebook`: entries below 512 name a row of the voxel's own device, entries 512 + q * 4 + i name slot i pulled from device q, and the largest value means no neighbour; offset 27 // 2 always names the voxel itself. `border`: each device's entries are distinct rows of its own block.
All inputs are finite; a program needn't handle non-finite values.
Results may differ from the reference program's by a relative error of at most 0.0041.
Values may be sent and summed in bfloat16 or wider, within the bound.
No kernel may reach another device: no remote copies, remote signals or barrier semaphores. Data moves between devices by JAX's collectives and lax.ppermute only.
A program may use at most 64 MiB of HBM per device.

```python
import jax
import jax.numpy as jnp
from jax import lax

C = 256
K = 27
MB = 2
CAP = 4
ROWS_DEV = 512
BORDER = 64
ROWS = 8192
N_SPACE = 16


def draw_features(key, part):
    key_base, key_rows, key_cols = jax.random.split(key, 3)
    base = jnp.clip(jax.random.normal(key_base, (MB, ROWS, C)), -5.0, 5.0)
    row_scale = jnp.exp(jax.random.uniform(key_rows, (MB, ROWS, 1), minval=jnp.log(0.3), maxval=jnp.log(3.0)))
    col_scale = jnp.exp(jax.random.uniform(key_cols, (1, 1, C), minval=jnp.log(0.3), maxval=jnp.log(3.0)))
    return (base * row_scale * col_scale).astype(jnp.bfloat16)


def draw_rulebook(key, part):
    key_kind, key_local, key_remote = jax.random.split(key, 3)
    kind = jax.random.randint(key_kind, (ROWS, K), 0, 10)
    local_code = jax.random.randint(key_local, (ROWS, K), 0, ROWS_DEV)
    remote_code = ROWS_DEV + jax.random.randint(key_remote, (ROWS, K), 0, N_SPACE * CAP)
    missing = jnp.full((ROWS, K), ROWS_DEV + N_SPACE * CAP, jnp.int32)
    code = jnp.where(kind < 5, local_code, jnp.where(kind < 8, remote_code, missing))
    own_row = (jnp.arange(ROWS, dtype=jnp.int32) % ROWS_DEV)[:, None]
    centre = (jnp.arange(K) == K // 2)[None, :]
    return jnp.where(centre, own_row, code).astype(jnp.int32)


def draw_border(key, part):
    device_keys = jax.random.split(key, N_SPACE)

    def one_device(device_key):
        return jax.random.permutation(device_key, ROWS_DEV)[:BORDER]
    return jax.vmap(one_device)(device_keys).astype(jnp.int32)


def place_ends(drawn, rng, low, largest):
    place = [jax.random.randint(jax.random.fold_in(rng, axis), (), 0, length) for axis, length in enumerate(drawn.shape)]
    widest = drawn.shape.index(max(drawn.shape))
    beside = place[:widest] + [(place[widest] + 1) % drawn.shape[widest]] + place[widest + 1:]
    return drawn.at[tuple(place)].set(low).at[tuple(beside)].set(largest)


def shard_levels(stream_key, extent, pieces, least, largest):
    def one(axis_at, shards_of):
        heights = jax.random.uniform(jax.random.fold_in(jax.random.fold_in(stream_key, 6), axis_at), (shards_of,), jnp.float32, least / len(pieces), largest / len(pieces))
        return jnp.repeat(jnp.exp(heights), extent[axis_at] // shards_of).reshape((-1,) + (1,) * (len(extent) - axis_at - 1))

    gain = one(*pieces[0])
    for cut in pieces[1:]:
        gain = gain * one(*cut)
    return gain


def centred(key, extent, scale, reach, pieces=(), kind=jnp.bfloat16):
    loudness = shard_levels(key, extent, pieces, -0.22, 0.18) if pieces else 1.0
    entries = jax.random.normal(key, extent, jnp.float32) * scale * loudness
    return jnp.minimum(jnp.maximum(entries, -reach), reach).astype(kind)


def setup_inputs(seed: int = 0) -> dict:
    streams_of = jax.random.split(jax.random.key(seed), 7)
    features = draw_features(jax.random.fold_in(streams_of[6], 71), 0)
    weights = centred(streams_of[1], (2, K, C, C), (K * C) ** -0.5, 0.078125, ((0, 2),))
    conv_bias = centred(streams_of[2], (2, C), 1.0, 4.0, (), jnp.float32)
    rulebook = draw_rulebook(jax.random.fold_in(streams_of[6], 71), 0)
    border = draw_border(jax.random.fold_in(streams_of[6], 71), 0)
    pull_slots = place_ends(jax.random.randint(streams_of[5], (N_SPACE, N_SPACE, CAP), 0, BORDER), jax.random.fold_in(streams_of[5], 1), 0, BORDER - 1).astype(jnp.int32)
    return dict(features=features, weights=weights, conv_bias=conv_bias, rulebook=rulebook, border=border, pull_slots=pull_slots)


def global_rows(rulebook, border, pull_slots):
    owner = (jnp.arange(ROWS, dtype=jnp.int32) // ROWS_DEV)[:, None]
    local_rows = owner * ROWS_DEV + rulebook
    remote_code = jnp.clip(rulebook - ROWS_DEV, 0, N_SPACE * CAP - 1).astype(jnp.int32)
    peer_index = remote_code // CAP
    slot_index = remote_code % CAP
    chosen = pull_slots[owner, peer_index, slot_index]
    remote_rows = peer_index * ROWS_DEV + border[peer_index, chosen]
    missing = jnp.full_like(rulebook, ROWS)
    return jnp.where(rulebook < ROWS_DEV, local_rows, jnp.where(rulebook < ROWS_DEV + N_SPACE * CAP, remote_rows, missing)).astype(jnp.int32)

def section(inputs, kernel, bias_row, neighbour):
    values = inputs.astype(jnp.float32)
    mean_square = lax.optimization_barrier(jnp.mean(values * values, axis=1, keepdims=True))
    normed = (values * lax.rsqrt(mean_square + 1e-06)).astype(jnp.bfloat16)
    extended = jnp.concatenate([normed, jnp.zeros((1, C), jnp.bfloat16)], axis=0)

    def add_offset(total, item):
        column, matrix = item
        return (total + jnp.dot(extended[column], matrix, preferred_element_type=jnp.float32), None)
    convolved, unused = lax.scan(add_offset, jnp.zeros((ROWS, C), jnp.float32), (neighbour.T, kernel))
    return (values + jax.nn.silu(convolved + bias_row)).astype(jnp.bfloat16)

def reference(features, weights, conv_bias, rulebook, border, pull_slots):
    neighbour = global_rows(rulebook, border, pull_slots)
    latents = []
    recons = []
    for batch_index in range(MB):
        latent = section(features[batch_index], weights[0], conv_bias[0], neighbour)
        latents.append(latent)
        recons.append(section(latent, weights[1], conv_bias[1], neighbour))
    return jnp.stack([jnp.stack(latents), jnp.stack(recons)])
```

```python
import functools

import jax
import jax.numpy as jnp
from jax import lax
from jax.experimental import pallas as pl
from jax.experimental.pallas import tpu as pltpu
from jax.sharding import PartitionSpec as P

BF16 = jnp.bfloat16
F32 = jnp.float32
I32 = jnp.int32
AUX = 16
CHUNK = 3
VMEM_BYTES = 60 * 2**20


def iota(shape, dim):
    return lax.broadcasted_iota(I32, shape, dim)


def onehot(column, width):
    return (column == iota((column.shape[0], width), 1)).astype(BF16)


def dot(a, b):
    return jnp.dot(a, b, preferred_element_type=F32)


def normalise(values):
    mean_square = jnp.mean(values * values, axis=1, keepdims=True)
    return (values * lax.rsqrt(mean_square + 1e-06)).astype(BF16)


def row_to_column(row):
    n = row.shape[1]
    spread = jnp.where(iota((n, n), 0) == iota((n, n), 1), row.astype(F32), 0.0)
    return jnp.sum(spread, axis=1, keepdims=True).astype(I32)


def pick_lane(table, lane):
    kept = jnp.where(iota(table.shape, 1) == lane, table, 0.0)
    return jnp.sum(kept, axis=1, keepdims=True).astype(I32)


def slot_numbers(peers, cap):
    row = iota((peers * cap, 1), 0)
    peer = lax.div(row, cap)
    return peer, row - peer * cap


def prepare_kernel(phase_ref, features_ref, border_ref, wanted_ref, normed_ref, payload_ref, aux_ref):
    normed = normalise(features_ref[0].astype(F32))
    normed_ref[...] = normed
    peers, cap = wanted_ref.shape[1:]
    borders = border_ref.shape[1]
    stride = borders + AUX
    rows = dot(onehot(row_to_column(border_ref[...]), normed.shape[0]), normed).astype(BF16)
    aux_ref[...] = jnp.zeros_like(aux_ref)
    aux_ref[:, 0:cap] = wanted_ref[0].astype(F32)
    for peer in range(peers):
        payload_ref[peer * stride : peer * stride + borders, :] = rows
        own = jnp.broadcast_to(aux_ref[peer : peer + 1, :], (AUX, aux_ref.shape[1]))
        payload_ref[peer * stride + borders : (peer + 1) * stride, :] = own.astype(BF16)


def load_weights(section, phase_ref, own_ref, other_ref, held_ref, sems):
    offsets = held_ref.shape[0]
    chunks = [(c, min(CHUNK, offsets - c)) for c in range(0, offsets, CHUNK)]

    def copies(source):
        return [
            pltpu.make_async_copy(source.at[pl.ds(first, count)], held_ref.at[pl.ds(first, count)], sems.at[at])
            for at, (first, count) in enumerate(chunks)
        ]

    @pl.when(phase_ref[0] == section)
    def _():
        for copy in copies(own_ref):
            copy.start()

    @pl.when(phase_ref[0] != section)
    def _():
        for copy in copies(other_ref):
            copy.start()

    return chunks, [copy.wait for copy in copies(own_ref)]


def local_kernel(section, phase_ref, codes_ref, normed_ref, own_ref, other_ref, total_ref, held_ref, sems):
    chunks, waits = load_weights(section, phase_ref, own_ref, other_ref, held_ref, sems)
    rows, channels = normed_ref.shape
    normed = normed_ref[...]
    total = None
    for at, (first, count) in enumerate(chunks):
        picked = [
            dot(onehot(codes_ref[:, k : k + 1], rows), normed).astype(BF16) for k in range(first, first + count)
        ]
        waits[at]()
        matrix = held_ref[first : first + count].reshape(count * channels, channels)
        term = dot(jnp.concatenate(picked, axis=1), matrix)
        total = term if total is None else total + term
    total_ref[...] = total


def halo_term(chunks, waits, codes_ref, halo, held_ref, spread_ref):
    rows, offsets = codes_ref.shape
    channels = halo.shape[1]
    slots = halo.shape[0]
    pack = 128 // slots if slots < 128 else 1
    width = slots * pack
    groups = -(-offsets // pack)
    for k in range(offsets, groups * pack):
        spread_ref[k * slots : (k + 1) * slots, :] = jnp.zeros((slots, channels), BF16)
    lane = iota((rows, width), 1)
    pieces = []
    for group in range(groups):
        wanted = None
        for j in range(pack):
            k = group * pack + j
            code = codes_ref[:, k : k + 1] + (j * slots - rows) if k < offsets else jnp.full((rows, 1), -1, I32)
            code = jnp.broadcast_to(code, (rows, width))
            wanted = code if wanted is None else jnp.where(lane >= j * slots, code, wanted)
        pieces.append((wanted == lane).astype(BF16))
    for at, (first, count) in enumerate(chunks):
        waits[at]()
        for k in range(first, first + count):
            spread_ref[k * slots : (k + 1) * slots, :] = dot(halo, held_ref[k]).astype(BF16)
    return dot(jnp.concatenate(pieces, axis=1), spread_ref[...])


def residual(values, convolved):
    return (values + jax.nn.silu(convolved)).astype(BF16)


def encode_kernel(
    phase_ref, features_ref, total_ref, codes_ref, received_ref, border_ref, wanted_ref, bias_ref, own_ref, other_ref,
    latent_ref, normed_ref, send_ref, held_ref, spread_ref, aux_ref, sems,
):
    chunks, waits = load_weights(0, phase_ref, own_ref, other_ref, held_ref, sems)
    rows = codes_ref.shape[0]
    peers, cap = wanted_ref.shape[1:]
    borders = border_ref.shape[1]
    stride = borders + AUX
    peer, slot = slot_numbers(peers, cap)
    aux_ref[...] = jnp.zeros_like(aux_ref)
    aux_ref[:, 0:cap] = wanted_ref[0].astype(F32)
    mine = pick_lane(dot(onehot(peer, peers), aux_ref[...].astype(BF16)), slot)
    places = jnp.concatenate([peer * stride + mine, peer * stride + borders], axis=0)
    found = dot(onehot(places, peers * stride), received_ref[...])
    halo = found[: peers * cap].astype(BF16)
    theirs = pick_lane(found[peers * cap :, 0:128], slot)
    asked = pick_lane(jnp.broadcast_to(border_ref[...].astype(F32), (peers * cap, borders)), theirs)

    convolved = total_ref[...] + halo_term(chunks, waits, codes_ref, halo, held_ref, spread_ref) + bias_ref[0:1, :]
    latent = residual(features_ref[0].astype(F32), convolved)
    latent_ref[...] = latent
    normed = normalise(latent.astype(F32))
    normed_ref[...] = normed
    doubled = iota((2 * peers * cap, 1), 0)
    which = lax.div(doubled, 2)
    out = dot(onehot(asked, rows), normed).astype(BF16)
    half = out.shape[1] // 2
    pair = onehot(which, peers * cap)
    left = dot(pair, out[:, :half])
    right = dot(pair, out[:, half:])
    send_ref[...] = jnp.where(doubled - 2 * which == 0, left, right).astype(BF16)


def decode_kernel(
    phase_ref, latent_ref, total_ref, codes_ref, received_ref, bias_ref, own_ref, other_ref,
    out_ref, held_ref, spread_ref, sems,
):
    chunks, waits = load_weights(1, phase_ref, own_ref, other_ref, held_ref, sems)
    received = received_ref[...]
    slots = received.shape[0] // 2
    even = 2 * iota((slots, 1), 0)
    halves = [dot(onehot(even + j, 2 * slots), received).astype(BF16) for j in range(2)]
    halo = jnp.concatenate(halves, axis=1)
    convolved = total_ref[...] + halo_term(chunks, waits, codes_ref, halo, held_ref, spread_ref) + bias_ref[1:2, :]
    out_ref[...] = residual(latent_ref[...].astype(F32), convolved)


def body(features, weights, conv_bias, rulebook, border, pull_slots):
    phase = lax.axis_index("phase")
    micro, rows, channels = features.shape
    peers, cap = pull_slots.shape[1:]
    borders = border.shape[1]
    stride = borders + AUX
    offsets = rulebook.shape[1]
    slots = peers * cap
    pack = 128 // slots if slots < 128 else 1
    spread_rows = -(-offsets // pack) * pack * slots
    phase_row = phase.astype(I32).reshape(1)
    own = weights[0]
    swap = [(0, 1), (1, 0)]
    other = lax.ppermute(own, "phase", swap)

    whole = lambda *shape: pl.BlockSpec(shape, lambda i, p: (0,) * len(shape))
    mine = pl.BlockSpec((1, rows, channels), lambda i, p: (p[0], 0, 0))
    anywhere = pl.BlockSpec(memory_space=pl.ANY)
    block = jax.ShapeDtypeStruct((rows, channels), BF16)
    chunk_count = -(-offsets // CHUNK)
    held = [pltpu.VMEM((offsets, channels, channels), BF16)]
    spread = [pltpu.VMEM((spread_rows, channels), BF16)]
    aux = [pltpu.VMEM((peers, 128), F32)]
    sems = [pltpu.SemaphoreType.DMA((chunk_count,))]

    def call(kernel, name, in_specs, out_specs, out_shape, scratch, flops):
        return pl.pallas_call(
            kernel,
            grid_spec=pltpu.PrefetchScalarGridSpec(
                num_scalar_prefetch=1, grid=(1,), in_specs=in_specs, out_specs=out_specs, scratch_shapes=scratch
            ),
            out_shape=out_shape,
            compiler_params=pltpu.CompilerParams(vmem_limit_bytes=VMEM_BYTES),
            cost_estimate=pl.CostEstimate(flops=flops, bytes_accessed=offsets * channels * channels * 2, transcendentals=0),
            name=name,
        )

    normed, payload = call(
        prepare_kernel, "prepare",
        [mine, whole(1, borders), whole(1, peers, cap)],
        [whole(rows, channels), whole(peers * stride, channels)],
        [block, jax.ShapeDtypeStruct((peers * stride, channels), BF16)],
        [pltpu.VMEM((peers, channels), F32)], 10**8,
    )(phase_row, features, border, pull_slots)
    received = lax.all_to_all(payload, "space", 0, 0, tiled=True)

    def local(section, normed):
        return call(
            functools.partial(local_kernel, section), "local",
            [whole(rows, offsets), whole(rows, channels), anywhere, anywhere],
            whole(rows, channels), jax.ShapeDtypeStruct((rows, channels), F32),
            held + sems, 2 * offsets * rows * channels * (rows + channels),
        )(phase_row, rulebook, normed, own, other)

    total = local(0, normed)
    latent, normed, send = call(
        encode_kernel, "encode",
        [mine, whole(rows, channels), whole(rows, offsets), whole(peers * stride, channels), whole(1, borders),
         whole(1, peers, cap), whole(2, channels), anywhere, anywhere],
        [whole(rows, channels), whole(rows, channels), whole(2 * slots, channels // 2)],
        [block, block, jax.ShapeDtypeStruct((2 * slots, channels // 2), BF16)],
        held + spread + aux + sems, 10**9,
    )(phase_row, features, total, rulebook, received, border, pull_slots, conv_bias, own, other)
    received = lax.all_to_all(send, "space", 0, 0, tiled=True)
    total = local(1, normed)
    recon = call(
        decode_kernel, "decode",
        [whole(rows, channels), whole(rows, channels), whole(rows, offsets), whole(2 * slots, channels // 2),
         whole(2, channels), anywhere, anywhere],
        whole(rows, channels), block, held + spread + sems, 10**9,
    )(phase_row, latent, total, rulebook, received, conv_bias, own, other)

    latent_there = lax.ppermute(latent, "phase", [(1, 0)])
    recon_there = lax.ppermute(recon, "phase", [(0, 1)])
    return jnp.where(
        phase == 0, jnp.stack([latent, latent_there]), jnp.stack([recon_there, recon])
    )[None]


def solution(mesh):
    return jax.shard_map(
        body,
        mesh=mesh,
        in_specs=(
            P(None, "space", None),
            P("phase", None, None, None),
            P(),
            P("space", None),
            P("space", None),
            P("space", None, None),
        ),
        out_specs=P("phase", None, "space", None),
        check_vma=False,
    )
```

```python
import functools

import jax
import jax.numpy as jnp
from jax import lax
from jax.experimental import pallas as pl
from jax.experimental.pallas import tpu as pltpu
from jax.sharding import PartitionSpec as P

BF16 = jnp.bfloat16
F32 = jnp.float32
I32 = jnp.int32
TILE = 8
CHUNK = 3
VMEM_BYTES = 24 * 2**20


def iota(shape, dim):
    return lax.broadcasted_iota(I32, shape, dim)


def onehot(column, width):
    return (column == iota((column.shape[0], width), 1)).astype(BF16)


def dot(a, b):
    return jnp.dot(a, b, preferred_element_type=F32)


def normalise(values):
    mean_square = jnp.mean(values * values, axis=1, keepdims=True)
    return (values * lax.rsqrt(mean_square + 1e-06)).astype(BF16)


def packing(slots, offsets):
    pack = 128 // slots if slots < 128 else 1
    return pack, -(-offsets // pack)


def ask_kernel(wanted_ref, ask_ref):
    cap, peers = wanted_ref.shape
    for peer in range(peers):
        column = jnp.broadcast_to(wanted_ref[:, peer : peer + 1], (cap, 128))
        for at in range(0, TILE, cap):
            ask_ref[peer * TILE + at : peer * TILE + at + cap, :] = column


def build_halo_onehot(codes_ref, halo_onehot_ref, slots):
    rows, offsets = codes_ref.shape
    pack, groups = packing(slots, offsets)
    width = slots * pack
    lane = iota((rows, width), 1)
    for group in range(groups):
        named = None
        for j in range(pack):
            k = group * pack + j
            code = codes_ref[:, k : k + 1] + (j * slots - rows) if k < offsets else jnp.full((rows, 1), -1, I32)
            code = jnp.broadcast_to(code, (rows, width))
            named = code if named is None else jnp.where(lane >= j * slots, code, named)
        halo_onehot_ref[:, group * width : (group + 1) * width] = (named == lane).astype(BF16)


def send_kernel(normed_ref, asked_ref, border_ref, send_ref):
    send_ref[...] = wanted_rows(normed_ref[...], asked_ref, border_ref)


def wanted_rows(normed, asked_ref, border_ref):
    requests, borders = asked_ref.shape[0], border_ref.shape[1]
    named = asked_ref[:, 0:1] == iota((requests, borders), 1)
    places = jnp.where(named, jnp.broadcast_to(border_ref[...].astype(F32), (requests, borders)), 0.0)
    place = jnp.sum(places, axis=1, keepdims=True).astype(I32)
    return dot(onehot(place, normed.shape[0]), normed).astype(BF16)


def local_kernel(section, phase_ref, codes_ref, normed_ref, own_ref, other_ref, total_ref):
    rows, channels = normed_ref.shape
    offsets = codes_ref.shape[1]

    def convolve(weights_ref):
        normed = normed_ref[...]
        total = None
        for first in range(0, offsets, CHUNK):
            count = min(CHUNK, offsets - first)
            picked = [
                dot(onehot(codes_ref[:, k : k + 1], rows), normed).astype(BF16) for k in range(first, first + count)
            ]
            matrix = weights_ref[first : first + count].reshape(count * channels, channels)
            term = dot(jnp.concatenate(picked, axis=1), matrix)
            total = term if total is None else total + term
        total_ref[...] = total

    pl.when(phase_ref[0] == section)(lambda: convolve(own_ref))
    pl.when(phase_ref[0] != section)(lambda: convolve(other_ref))


def halo_term(section, phase_ref, received_ref, cap, halo_onehot_ref, own_ref, other_ref, spread_ref):
    offsets, channels = own_ref.shape[:2]
    requests = received_ref.shape[0]
    slots = requests // TILE * cap
    pack, groups = packing(slots, offsets)
    row = iota((slots, 1), 0)
    peer = lax.div(row, cap)
    halo = dot(onehot(peer * TILE + row - peer * cap, requests), received_ref[...]).astype(BF16)
    for k in range(offsets, groups * pack):
        spread_ref[k * slots : (k + 1) * slots, :] = jnp.zeros((slots, channels), BF16)

    def spread(weights_ref):
        for k in range(offsets):
            spread_ref[k * slots : (k + 1) * slots, :] = dot(halo, weights_ref[k]).astype(BF16)

    pl.when(phase_ref[0] == section)(lambda: spread(own_ref))
    pl.when(phase_ref[0] != section)(lambda: spread(other_ref))
    whole = groups * pack * slots
    step = 2048 if whole > 2048 else whole
    total = None
    for first in range(0, whole, step):
        last = min(first + step, whole)
        term = dot(halo_onehot_ref[:, first:last], spread_ref[first:last, :])
        total = term if total is None else total + term
    return total


def residual(values, convolved):
    return (values + jax.nn.silu(convolved)).astype(BF16)


def encode_kernel(
    cap, phase_ref, features_ref, total_ref, received_ref, halo_onehot_ref, asked_ref, border_ref, bias_ref,
    own_ref, other_ref, latent_ref, normed_ref, send_ref, spread_ref,
):
    term = halo_term(0, phase_ref, received_ref, cap, halo_onehot_ref, own_ref, other_ref, spread_ref)
    latent = residual(features_ref[phase_ref[0]].astype(F32), total_ref[...] + term + bias_ref[0:1, :])
    latent_ref[...] = latent
    normed = normalise(latent.astype(F32))
    normed_ref[...] = normed
    send_ref[...] = wanted_rows(normed, asked_ref, border_ref)


def decode_kernel(
    cap, phase_ref, latent_ref, total_ref, received_ref, halo_onehot_ref, bias_ref, own_ref, other_ref,
    kept_ref, passed_ref, spread_ref,
):
    term = halo_term(1, phase_ref, received_ref, cap, halo_onehot_ref, own_ref, other_ref, spread_ref)
    latent = latent_ref[...]
    recon = residual(latent.astype(F32), total_ref[...] + term + bias_ref[1:2, :])
    first = phase_ref[0] == 0
    kept_ref[phase_ref[0]] = jnp.where(first, latent, recon)
    passed_ref[...] = jnp.where(first, recon, latent)


def body(features, weights, conv_bias, rulebook, border, pull_slots):
    phase = lax.axis_index("phase").astype(I32)
    micro, rows, channels = features.shape
    peers, cap = pull_slots.shape[1:]
    offsets = rulebook.shape[1]
    slots = peers * cap
    pack, groups = packing(slots, offsets)
    spread_rows = groups * pack * slots
    phase_row = phase.reshape(1)
    own = weights[0]
    swap = [(0, 1), (1, 0)]
    other = lax.ppermute(own, "phase", swap)

    vmem = pl.BlockSpec(memory_space=pltpu.VMEM)
    smem = pl.BlockSpec(memory_space=pltpu.SMEM)
    block = jax.ShapeDtypeStruct((rows, channels), BF16)
    sent = jax.ShapeDtypeStruct((peers * TILE, channels), BF16)
    spread = [pltpu.VMEM((spread_rows, channels), BF16)]

    def call(kernel, name, in_specs, out_shape, flops, scratch=()):
        single = isinstance(out_shape, jax.ShapeDtypeStruct)
        return pl.pallas_call(
            kernel,
            in_specs=in_specs,
            out_specs=vmem if single else [vmem] * len(out_shape),
            out_shape=out_shape,
            scratch_shapes=list(scratch),
            compiler_params=pltpu.CompilerParams(vmem_limit_bytes=VMEM_BYTES),
            cost_estimate=pl.CostEstimate(flops=flops, bytes_accessed=10**6, transcendentals=0),
            name=name,
        )

    def exchange(value):
        return lax.all_to_all(value, "space", 0, 0, tiled=True)

    ask = call(ask_kernel, "ask", [vmem], jax.ShapeDtypeStruct((peers * TILE, 128), I32), 10**6)(pull_slots[0].T)
    asked = exchange(ask)

    def prepare(phase_ref, features_ref, codes_ref, normed_ref, halo_onehot_ref):
        normed_ref[...] = normalise(features_ref[phase_ref[0]].astype(F32))
        build_halo_onehot(codes_ref, halo_onehot_ref, slots)

    normed, halo_onehot = call(
        prepare, "prepare", [smem, vmem, vmem],
        [block, jax.ShapeDtypeStruct((rows, spread_rows), BF16)], 10**9,
    )(phase_row, features, rulebook)
    send = call(send_kernel, "send", [vmem] * 3, sent, 10**8)(normed, asked, border)
    received = exchange(send)

    def local(section, normed):
        return call(
            functools.partial(local_kernel, section), "local", [smem] + [vmem] * 4,
            jax.ShapeDtypeStruct((rows, channels), F32), 2 * offsets * rows * channels * (rows + channels),
        )(phase_row, rulebook, normed, own, other)

    total = local(0, normed)
    latent, normed, send = call(
        functools.partial(encode_kernel, cap), "encode", [smem] + [vmem] * 9, [block, block, sent], 10**9, spread
    )(phase_row, features, total, received, halo_onehot, asked, border, conv_bias, own, other)
    received = exchange(send)
    total = local(1, normed)
    kept, passed = call(
        functools.partial(decode_kernel, cap), "decode", [smem] + [vmem] * 7,
        [jax.ShapeDtypeStruct((2, rows, channels), BF16), block], 10**9, spread,
    )(phase_row, latent, total, received, halo_onehot, conv_bias, own, other)
    got = lax.ppermute(passed, "phase", swap)
    return lax.dynamic_update_slice(kept, got[None], (1 - phase, 0, 0))[None]


def solution(mesh):
    return jax.shard_map(
        body,
        mesh=mesh,
        in_specs=(
            P(None, "space", None),
            P("phase", None, None, None),
            P(),
            P("space", None),
            P("space", None),
            P("space", None, None),
        ),
        out_specs=P("phase", None, "space", None),
        check_vma=False,
    )
```

```python
import functools

import jax
import jax.numpy as jnp
from jax import lax
from jax.experimental import pallas as pl
from jax.experimental.pallas import tpu as pltpu
from jax.sharding import PartitionSpec as P

BF16 = jnp.bfloat16
F32 = jnp.float32
I32 = jnp.int32
TILE = 8
CHUNK = 9
VMEM_BYTES = 60 * 2**20


def iota(shape, dim):
    return lax.broadcasted_iota(I32, shape, dim)


def onehot(column, width):
    return (column == iota((column.shape[0], width), 1)).astype(BF16)


def dot(a, b):
    return jnp.dot(a, b, preferred_element_type=F32)


def normalise(values):
    mean_square = jnp.mean(values * values, axis=1, keepdims=True)
    return (values * lax.rsqrt(mean_square + 1e-06)).astype(BF16)


def packing(slots, offsets):
    pack = 128 // slots if slots < 128 else 1
    return pack, -(-offsets // pack)


def lookup(column, row):
    shape = (column.shape[0], row.shape[1])
    named = jnp.where(column == iota(shape, 1), jnp.broadcast_to(row.astype(F32), shape), 0.0)
    return jnp.sum(named, axis=1, keepdims=True).astype(I32)


class Copies:
    def __init__(self, sems):
        self.sems = sems
        self.used = 0

    def start(self, source, target):
        copy = pltpu.make_async_copy(source, target, self.sems.at[self.used])
        self.used += 1
        copy.start()
        return copy

    def weights(self, section, phase, own_ref, other_ref, held_ref):
        offsets = held_ref.shape[0]
        spans = [(first, min(CHUNK, offsets - first)) for first in range(0, offsets, CHUNK)]
        base = self.used
        self.used += len(spans)

        def copies(source):
            return [
                pltpu.make_async_copy(source.at[pl.ds(first, n)], held_ref.at[pl.ds(first, n)], self.sems.at[base + i])
                for i, (first, n) in enumerate(spans)
            ]

        pl.when(phase == section)(lambda: [copy.start() for copy in copies(own_ref)] and None)
        pl.when(phase != section)(lambda: [copy.start() for copy in copies(other_ref)] and None)
        return [(first, n, copy) for (first, n), copy in zip(spans, copies(own_ref))]


def publish_kernel(features_ref, border_ref, wanted_ref, payload_ref, block_ref, border_v, wanted_v, payload_v, sems):
    copies = Copies(sems)
    loads = [
        copies.start(features_ref.at[lax.axis_index("phase")], block_ref),
        copies.start(border_ref, border_v),
        copies.start(wanted_ref, wanted_v),
    ]
    for load in loads:
        load.wait()
    borders = border_v.shape[1]
    cap, peers = wanted_v.shape
    rows, channels = block_ref.shape
    place = lookup(iota((borders, 1), 0), border_v[...])
    picked = dot(onehot(place, rows), block_ref[...])
    shown = normalise(picked).astype(F32)
    stride = borders + TILE
    pad = jnp.zeros((TILE - cap, channels), F32)
    wanted = wanted_v[...].astype(F32)
    for peer in range(0, peers, 2):
        parts = []
        for each in (peer, peer + 1):
            parts += [shown, jnp.concatenate([jnp.broadcast_to(wanted[:, each : each + 1], (cap, channels)), pad], axis=0)]
        payload_v[peer * stride : (peer + 2) * stride, :] = jnp.concatenate(parts, axis=0).astype(BF16)
    copies.start(payload_v, payload_ref).wait()


def convolve(codes_ref, normed, held_ref, chunks):
    rows, channels = normed.shape
    total = None
    for first, count, copy in chunks:
        picked = [dot(onehot(codes_ref[:, k : k + 1], rows), normed).astype(BF16) for k in range(first, first + count)]
        copy.wait()
        matrix = held_ref[first : first + count].reshape(count * channels, channels)
        term = dot(jnp.concatenate(picked, axis=1), matrix)
        total = term if total is None else total + term
    return total


def slot_numbers(rows, per_peer, cap):
    row = iota((rows, 1), 0)
    peer = lax.div(row, per_peer)
    return peer, lax.rem(row - peer * per_peer, cap)


def build_halo_onehot(codes_ref, slots, halo_onehot_v):
    rows, offsets = codes_ref.shape
    pack, groups = packing(slots, offsets)
    width = slots * pack
    lane = iota((rows, width), 1)
    for group in range(groups):
        named = None
        for j in range(pack):
            k = group * pack + j
            code = codes_ref[:, k : k + 1] + (j * slots - rows) if k < offsets else jnp.full((rows, 1), -1, I32)
            code = jnp.broadcast_to(code, (rows, width))
            named = code if named is None else jnp.where(lane >= j * slots, code, named)
        halo_onehot_v[:, group * width : (group + 1) * width] = (named == lane).astype(BF16)


def published_places(wanted, borders):
    cap, peers = wanted.shape
    stride = borders + TILE
    peer, slot = slot_numbers(peers * cap, cap, cap)
    mine = lax.dot_general(
        onehot(peer, peers), wanted.astype(BF16), (((1,), (1,)), ((), ())), preferred_element_type=F32
    )
    mine = jnp.sum(jnp.where(iota(mine.shape, 1) == slot, mine, 0.0), axis=1, keepdims=True).astype(I32)
    asker, place = slot_numbers(peers * TILE, TILE, cap)
    return jnp.concatenate([peer * stride + mine, asker * stride + borders + place], axis=0)


def first_local_kernel(
    borders, features_ref, codes_ref, wanted_ref, own_ref, other_ref, total_ref, halo_onehot_ref, places_ref,
    block_ref, codes_v, wanted_v, held_ref, total_v, halo_onehot_v, places_v, sems,
):
    phase = lax.axis_index("phase")
    copies = Copies(sems)
    loads = [
        copies.start(codes_ref, codes_v),
        copies.start(features_ref.at[phase], block_ref),
        copies.start(wanted_ref, wanted_v),
    ]
    chunks = copies.weights(0, phase, own_ref, other_ref, held_ref)
    for load in loads:
        load.wait()
    cap, peers = wanted_v.shape
    places_v[...] = jnp.broadcast_to(published_places(wanted_v[...], borders), places_v.shape)
    build_halo_onehot(codes_v, peers * cap, halo_onehot_v)
    stores = [copies.start(places_v, places_ref), copies.start(halo_onehot_v, halo_onehot_ref)]
    total_v[...] = convolve(codes_v, normalise(block_ref[...].astype(F32)), held_ref, chunks)
    stores.append(copies.start(total_v, total_ref))
    for store in stores:
        store.wait()


def second_local_kernel(normed_ref, codes_ref, own_ref, other_ref, total_ref, block_ref, codes_v, held_ref, total_v, sems):
    phase = lax.axis_index("phase")
    copies = Copies(sems)
    loads = [copies.start(codes_ref, codes_v), copies.start(normed_ref, block_ref)]
    chunks = copies.weights(1, phase, own_ref, other_ref, held_ref)
    for load in loads:
        load.wait()
    total_v[...] = convolve(codes_v, block_ref[...], held_ref, chunks)
    copies.start(total_v, total_ref).wait()


def pick_rows(places, source_ref):
    rows = source_ref.shape[0]
    step = next(n for n in range(min(rows, 1536) // 16 * 16, 0, -16) if rows % n == 0)
    found = None
    for first in range(0, rows, step):
        term = dot(onehot(places - first, step), source_ref[first : first + step, :])
        found = term if found is None else found + term
    return found


def halo_term(halo, offsets, chunks, held_ref, spread_ref, halo_onehot_v, onehot_load):
    slots, channels = halo.shape
    pack, groups = packing(slots, offsets)
    whole = groups * pack * slots
    if whole > offsets * slots:
        spread_ref[offsets * slots : whole, :] = jnp.zeros((whole - offsets * slots, channels), BF16)
    for first, count, copy in chunks:
        copy.wait()
        for k in range(first, first + count):
            spread_ref[k * slots : (k + 1) * slots, :] = dot(halo, held_ref[k]).astype(BF16)
    onehot_load.wait()
    total = None
    for first in range(0, whole, 2048):
        last = min(first + 2048, whole)
        term = dot(halo_onehot_v[:, first:last], spread_ref[first:last, :])
        total = term if total is None else total + term
    return total


def residual(values, convolved):
    return (values + jax.nn.silu(convolved)).astype(BF16)


def encode_kernel(
    features_ref, total_ref, received_ref, halo_onehot_ref, places_ref, border_ref, bias_ref, own_ref, other_ref,
    latent_ref, normed_ref, send_ref,
    block_ref, total_v, received_v, halo_onehot_v, places_v, border_v, bias_v, held_ref, spread_ref,
    latent_v, normed_v, send_v, sems,
):
    phase = lax.axis_index("phase")
    copies = Copies(sems)
    early = [
        copies.start(received_ref, received_v),
        copies.start(places_ref, places_v),
        copies.start(border_ref, border_v),
    ]
    chunks = copies.weights(0, phase, own_ref, other_ref, held_ref)
    onehot_load = copies.start(halo_onehot_ref, halo_onehot_v)
    late = [
        copies.start(total_ref, total_v),
        copies.start(features_ref.at[phase], block_ref),
        copies.start(bias_ref, bias_v),
    ]
    for load in early:
        load.wait()
    requests = send_v.shape[0]
    slots = places_v.shape[0] - requests
    found = pick_rows(places_v[:, 0:1], received_v)
    asked = lookup(found[slots:, 0:1].astype(I32), border_v[...])
    term = halo_term(found[:slots].astype(BF16), held_ref.shape[0], chunks, held_ref, spread_ref, halo_onehot_v, onehot_load)
    for load in late:
        load.wait()
    latent = residual(block_ref[...].astype(F32), total_v[...] + term + bias_v[0:1, :])
    latent_v[...] = latent
    stores = [copies.start(latent_v, latent_ref)]
    normed = normalise(latent.astype(F32))
    normed_v[...] = normed
    stores.append(copies.start(normed_v, normed_ref))
    send_v[...] = dot(onehot(asked, normed.shape[0]), normed).astype(BF16)
    stores.append(copies.start(send_v, send_ref))
    for store in stores:
        store.wait()


def decode_kernel(
    cap, latent_ref, total_ref, received_ref, halo_onehot_ref, bias_ref, own_ref, other_ref,
    kept_ref, passed_ref,
    latent_v, total_v, received_v, halo_onehot_v, bias_v, held_ref, spread_ref, recon_v, sems,
):
    phase = lax.axis_index("phase")
    copies = Copies(sems)
    received_load = copies.start(received_ref, received_v)
    chunks = copies.weights(1, phase, own_ref, other_ref, held_ref)
    onehot_load = copies.start(halo_onehot_ref, halo_onehot_v)
    late = [
        copies.start(total_ref, total_v),
        copies.start(latent_ref, latent_v),
        copies.start(bias_ref, bias_v),
    ]
    received_load.wait()
    requests = received_v.shape[0]
    peer, slot = slot_numbers(requests // TILE * cap, cap, cap)
    halo = pick_rows(peer * TILE + slot, received_v).astype(BF16)
    term = halo_term(halo, held_ref.shape[0], chunks, held_ref, spread_ref, halo_onehot_v, onehot_load)
    for load in late:
        load.wait()
    recon_v[...] = residual(latent_v[...].astype(F32), total_v[...] + term + bias_v[1:2, :])
    stores = [(latent_v, kept_ref.at[0], recon_v, passed_ref), (recon_v, kept_ref.at[1], latent_v, passed_ref)]
    used = copies.used

    def put(kept, place, passed, target):
        return [
            pltpu.make_async_copy(kept, place, sems.at[used]),
            pltpu.make_async_copy(passed, target, sems.at[used + 1]),
        ]

    pl.when(phase == 0)(lambda: [copy.start() for copy in put(*stores[0])] and None)
    pl.when(phase != 0)(lambda: [copy.start() for copy in put(*stores[1])] and None)
    for copy in put(*stores[0]):
        copy.wait()


def body(features, weights, conv_bias, rulebook, border, pull_slots):
    micro, rows, channels = features.shape
    peers, cap = pull_slots.shape[1:]
    borders = border.shape[1]
    offsets = rulebook.shape[1]
    slots = peers * cap
    pack, groups = packing(slots, offsets)
    published = peers * (borders + TILE)
    phase = lax.axis_index("phase")
    wanted = pull_slots[0].T
    own = weights[0]
    swap = [(0, 1), (1, 0)]
    other = lax.ppermute(own, "phase", swap)

    anywhere = pl.BlockSpec(memory_space=pl.ANY)
    array = jax.ShapeDtypeStruct
    block = array((rows, channels), BF16)
    total_like = array((rows, channels), F32)
    published_like = array((published, channels), BF16)
    sent_like = array((peers * TILE, channels), BF16)
    onehot_like = array((rows, groups * pack * slots), BF16)
    places_like = array((slots + peers * TILE, 128), I32)
    weights_like = array(own.shape, BF16)
    spread_like = array((groups * pack * slots, channels), BF16)

    def call(kernel, name, args, out_shapes, scratch, flops):
        return pl.pallas_call(
            kernel,
            in_specs=[anywhere] * len(args),
            out_specs=[anywhere] * len(out_shapes),
            out_shape=out_shapes,
            scratch_shapes=[pltpu.VMEM(s.shape, s.dtype) for s in scratch] + [pltpu.SemaphoreType.DMA((20,))],
            compiler_params=pltpu.CompilerParams(vmem_limit_bytes=VMEM_BYTES),
            cost_estimate=pl.CostEstimate(flops=flops, bytes_accessed=10**6, transcendentals=0),
            name=name,
        )(*args)

    def exchange(value):
        return lax.all_to_all(value, "space", 0, 0, tiled=True)

    local_flops = 2 * offsets * rows * channels * (rows + channels)
    payload, = call(
        publish_kernel, "publish", (features, border, wanted), [published_like],
        [block, border, wanted, published_like], 10**8,
    )
    received = exchange(payload)
    total, halo_onehot, places = call(
        functools.partial(first_local_kernel, borders), "first_local", (features, rulebook, wanted, own, other),
        [total_like, onehot_like, places_like],
        [block, rulebook, wanted, weights_like, total_like, onehot_like, places_like], local_flops,
    )
    latent, normed, send = call(
        encode_kernel, "encode", (features, total, received, halo_onehot, places, border, conv_bias, own, other),
        [block, block, sent_like],
        [block, total_like, published_like, onehot_like, places_like, border, conv_bias, weights_like, spread_like,
         block, block, sent_like], 10**9,
    )
    received = exchange(send)
    total, = call(
        second_local_kernel, "second_local", (normed, rulebook, own, other), [total_like],
        [block, rulebook, weights_like, total_like], local_flops,
    )
    kept, passed = call(
        functools.partial(decode_kernel, cap), "decode", (latent, total, received, halo_onehot, conv_bias, own, other),
        [array((2, rows, channels), BF16), block],
        [block, total_like, sent_like, onehot_like, conv_bias, weights_like, spread_like, block], 10**9,
    )
    got = lax.ppermute(passed, "phase", swap)
    return lax.dynamic_update_slice(kept, got[None], (1 - phase, 0, 0))[None]


def solution(mesh):
    return jax.shard_map(
        body,
        mesh=mesh,
        in_specs=(
            P(None, "space", None),
            P("phase", None, None, None),
            P(),
            P("space", None),
            P("space", None),
            P("space", None, None),
        ),
        out_specs=P("phase", None, "space", None),
        check_vma=False,
    )
```

```python
import functools

import jax
import jax.numpy as jnp
from jax import lax
from jax.experimental import pallas as pl
from jax.experimental.pallas import tpu as pltpu
from jax.sharding import PartitionSpec as P

BF16 = jnp.bfloat16
F32 = jnp.float32
I32 = jnp.int32
TILE = 8
BLOCK = 128
VMEM_BYTES = 60 * 2**20


def iota(shape, dim):
    return lax.broadcasted_iota(I32, shape, dim)


def onehot(column, width):
    return (column == iota((column.shape[0], width), 1)).astype(BF16)


def dot(a, b):
    return jnp.dot(a, b, preferred_element_type=F32)


def normalise(values):
    mean_square = jnp.mean(values * values, axis=1, keepdims=True)
    return (values * lax.rsqrt(mean_square + 1e-06)).astype(BF16)


def packing(slots, offsets):
    pack = 128 // slots if slots < 128 else 1
    return pack, -(-offsets // pack)


def lookup(column, row):
    shape = (column.shape[0], row.shape[1])
    named = jnp.where(column == iota(shape, 1), jnp.broadcast_to(row.astype(F32), shape), 0.0)
    return jnp.sum(named, axis=1, keepdims=True).astype(I32)


class Copies:
    def __init__(self, sems):
        self.sems = sems
        self.used = 0

    def start(self, source, target):
        copy = pltpu.make_async_copy(source, target, self.sems.at[self.used])
        self.used += 1
        copy.start()
        return copy

    def start_either(self, chosen, copy, other):
        sem = self.sems.at[self.used]
        self.used += 1
        copy, other = (pltpu.make_async_copy(source, target, sem) for source, target in (copy, other))
        pl.when(chosen)(copy.start)
        pl.when(jnp.logical_not(chosen))(other.start)
        return copy


def publish_kernel(features_ref, border_ref, wanted_ref, payload_ref, block_ref, border_v, wanted_v, payload_v, sems):
    copies = Copies(sems)
    loads = [
        copies.start(features_ref.at[lax.axis_index("phase")], block_ref),
        copies.start(border_ref, border_v),
        copies.start(wanted_ref, wanted_v),
    ]
    for load in loads:
        load.wait()
    borders = border_v.shape[1]
    cap, peers = wanted_v.shape
    rows, channels = block_ref.shape
    place = lookup(iota((borders, 1), 0), border_v[...])
    picked = dot(onehot(place, rows), block_ref[...])
    shown = normalise(picked).astype(F32)
    stride = borders + TILE
    pad = jnp.zeros((TILE - cap, channels), F32)
    wanted = wanted_v[...].astype(F32)
    for peer in range(0, peers, 2):
        parts = []
        for each in (peer, peer + 1):
            parts += [shown, jnp.concatenate([jnp.broadcast_to(wanted[:, each : each + 1], (cap, channels)), pad], axis=0)]
        payload_v[peer * stride : (peer + 2) * stride, :] = jnp.concatenate(parts, axis=0).astype(BF16)
    copies.start(payload_v, payload_ref).wait()


def gather(codes, normed, picked_v, beside=lambda k: None):
    rows, channels = normed.shape
    for k in range(codes.shape[1]):
        picked_v[:, k * channels : (k + 1) * channels] = dot(onehot(codes[:, k : k + 1], rows), normed).astype(BF16)
        beside(k)


def convolved_blocks(picked_v, held_ref):
    rows = picked_v.shape[0]
    matrix = held_ref[...].reshape(picked_v.shape[1], held_ref.shape[2])
    for first in range(0, rows, BLOCK):
        span = pl.ds(first, BLOCK)
        yield span, dot(picked_v[span, :], matrix)


def slot_numbers(rows, per_peer, cap):
    row = iota((rows, 1), 0)
    peer = lax.div(row, per_peer)
    return peer, lax.rem(row - peer * per_peer, cap)


def halo_onehot_group(codes, slots, group, halo_onehot_v):
    rows, offsets = codes.shape
    pack, groups = packing(slots, offsets)
    width = slots * pack
    lane = iota((rows, width), 1)
    named = None
    for j in range(pack):
        k = group * pack + j
        code = codes[:, k : k + 1] + (j * slots - rows) if k < offsets else jnp.full((rows, 1), -1, I32)
        code = jnp.broadcast_to(code, (rows, width))
        named = code if named is None else jnp.where(lane >= j * slots, code, named)
    halo_onehot_v[:, group * width : (group + 1) * width] = (named == lane).astype(BF16)


def published_places(wanted, borders):
    cap, peers = wanted.shape
    stride = borders + TILE
    peer, slot = slot_numbers(peers * cap, cap, cap)
    mine = lax.dot_general(
        onehot(peer, peers), wanted.astype(BF16), (((1,), (1,)), ((), ())), preferred_element_type=F32
    )
    mine = jnp.sum(jnp.where(iota(mine.shape, 1) == slot, mine, 0.0), axis=1, keepdims=True).astype(I32)
    asker, place = slot_numbers(peers * TILE, TILE, cap)
    return jnp.concatenate([peer * stride + mine, asker * stride + borders + place], axis=0)


def first_local_kernel(
    borders, features_ref, codes_ref, wanted_ref, own_ref, other_ref,
    total_ref, halo_onehot_ref, places_ref,
    block_ref, codes_v, wanted_v, held_ref, picked_v, total_v, halo_onehot_v, places_v, sems,
):
    phase = lax.axis_index("phase")
    copies = Copies(sems)
    loads = [
        copies.start(codes_ref, codes_v),
        copies.start(features_ref.at[phase], block_ref),
        copies.start(wanted_ref, wanted_v),
    ]
    weights_load = copies.start_either(phase == 0, (own_ref, held_ref), (other_ref, held_ref))
    for load in loads:
        load.wait()
    codes = codes_v[...].T
    cap, peers = wanted_v.shape
    slots = peers * cap
    pack, groups = packing(slots, codes.shape[1])
    places_v[...] = jnp.broadcast_to(published_places(wanted_v[...], borders), places_v.shape)

    def beside(k):
        if k % pack == 0:
            halo_onehot_group(codes, slots, k // pack, halo_onehot_v)

    gather(codes, normalise(block_ref[...].astype(F32)), picked_v, beside)
    stores = [copies.start(places_v, places_ref), copies.start(halo_onehot_v, halo_onehot_ref)]
    weights_load.wait()
    for span, term in convolved_blocks(picked_v, held_ref):
        total_v[span, :] = term
        stores.append(copies.start(total_v.at[span], total_ref.at[span]))
    for store in stores:
        store.wait()


def pick_rows(places, source_ref):
    rows = source_ref.shape[0]
    step = next(n for n in range(min(rows, 1536) // 16 * 16, 0, -16) if rows % n == 0)
    found = None
    for first in range(0, rows, step):
        term = dot(onehot(places - first, step), source_ref[first : first + step, :])
        found = term if found is None else found + term
    return found


def spread_halo(halo, held_ref, spread_ref):
    slots, channels = halo.shape
    offsets = held_ref.shape[0]
    whole = spread_ref.shape[0]
    if whole > offsets * slots:
        spread_ref[offsets * slots : whole, :] = jnp.zeros((whole - offsets * slots, channels), BF16)
    for k in range(offsets):
        spread_ref[k * slots : (k + 1) * slots, :] = dot(halo, held_ref[k]).astype(BF16)


def halo_term(halo_onehot_v, span, spread_ref):
    total = None
    for first in range(0, spread_ref.shape[0], 2048):
        lanes = pl.ds(first, min(2048, spread_ref.shape[0] - first))
        term = dot(halo_onehot_v[span, lanes], spread_ref[lanes, :])
        total = term if total is None else total + term
    return total


def residual(values, convolved):
    return (values + jax.nn.silu(convolved)).astype(BF16)


def encode_kernel(
    features_ref, total_ref, received_ref, halo_onehot_ref, places_ref, border_ref, bias_ref, own_ref, other_ref,
    latent_ref, normed_ref, send_ref,
    block_ref, total_v, received_v, halo_onehot_v, places_v, border_v, bias_v, held_ref, spread_ref,
    latent_v, normed_v, send_v, sems,
):
    phase = lax.axis_index("phase")
    copies = Copies(sems)
    early = [
        copies.start(received_ref, received_v),
        copies.start(places_ref, places_v),
        copies.start(border_ref, border_v),
    ]
    weights_load = copies.start_either(phase == 0, (own_ref, held_ref), (other_ref, held_ref))
    late = [
        copies.start(halo_onehot_ref, halo_onehot_v),
        copies.start(total_ref, total_v),
        copies.start(features_ref.at[phase], block_ref),
        copies.start(bias_ref, bias_v),
    ]
    for load in early:
        load.wait()
    slots = places_v.shape[0] - send_v.shape[0]
    found = pick_rows(places_v[:, 0:1], received_v)
    asked = lookup(found[slots:, 0:1].astype(I32), border_v[...])
    weights_load.wait()
    spread_halo(found[:slots].astype(BF16), held_ref, spread_ref)
    for load in late:
        load.wait()
    term = halo_term(halo_onehot_v, pl.ds(0, block_ref.shape[0]), spread_ref)
    latent = residual(block_ref[...].astype(F32), total_v[...] + term + bias_v[0:1, :])
    latent_v[...] = latent
    stores = [copies.start(latent_v, latent_ref)]
    normed = normalise(latent.astype(F32))
    normed_v[...] = normed
    stores.append(copies.start(normed_v, normed_ref))
    send_v[...] = dot(onehot(asked, normed.shape[0]), normed).astype(BF16)
    stores.append(copies.start(send_v, send_ref))
    for store in stores:
        store.wait()


def second_local_kernel(
    normed_ref, codes_ref, own_ref, other_ref, total_ref, normed_v, codes_v, held_ref, picked_v, total_v, sems
):
    phase = lax.axis_index("phase")
    copies = Copies(sems)
    early = [copies.start(codes_ref, codes_v), copies.start(normed_ref, normed_v)]
    weights_load = copies.start_either(phase == 1, (own_ref, held_ref), (other_ref, held_ref))
    for load in early:
        load.wait()
    gather(codes_v[...].T, normed_v[...], picked_v)
    weights_load.wait()
    stores = []
    for span, term in convolved_blocks(picked_v, held_ref):
        total_v[span, :] = term
        stores.append(copies.start(total_v.at[span], total_ref.at[span]))
    for store in stores:
        store.wait()


def decode_kernel(
    cap, latent_ref, total_ref, received_ref, halo_onehot_ref, bias_ref, own_ref, other_ref, kept_ref, passed_ref,
    latent_v, total_v, received_v, halo_onehot_v, bias_v, held_ref, spread_ref, recon_v, sems,
):
    first = lax.axis_index("phase") == 0
    copies = Copies(sems)
    received_load = copies.start(received_ref, received_v)
    weights_load = copies.start_either(first, (other_ref, held_ref), (own_ref, held_ref))
    late = [
        copies.start(halo_onehot_ref, halo_onehot_v),
        copies.start(total_ref, total_v),
        copies.start(latent_ref, latent_v),
        copies.start(bias_ref, bias_v),
    ]
    received_load.wait()
    peer, slot = slot_numbers(received_v.shape[0] // TILE * cap, cap, cap)
    halo = pick_rows(peer * TILE + slot, received_v).astype(BF16)
    weights_load.wait()
    spread_halo(halo, held_ref, spread_ref)
    for load in late:
        load.wait()
    stores = [copies.start_either(first, (latent_v, kept_ref.at[0]), (latent_v, passed_ref))]
    term = halo_term(halo_onehot_v, pl.ds(0, latent_v.shape[0]), spread_ref)
    recon_v[...] = residual(latent_v[...].astype(F32), total_v[...] + term + bias_v[1:2, :])
    stores.append(copies.start_either(first, (recon_v, passed_ref), (recon_v, kept_ref.at[1])))
    for store in stores:
        store.wait()


def body(features, weights, conv_bias, rulebook, border, pull_slots):
    micro, rows, channels = features.shape
    peers, cap = pull_slots.shape[1:]
    borders = border.shape[1]
    offsets = rulebook.shape[1]
    slots = peers * cap
    pack, groups = packing(slots, offsets)
    published = peers * (borders + TILE)
    phase = lax.axis_index("phase")
    wanted = pull_slots[0].T
    codes = rulebook.T
    own = weights[0]
    swap = [(0, 1), (1, 0)]
    other = lax.ppermute(own, "phase", swap)

    anywhere = pl.BlockSpec(memory_space=pl.ANY)
    array = jax.ShapeDtypeStruct
    block = array((rows, channels), BF16)
    total_like = array((rows, channels), F32)
    published_like = array((published, channels), BF16)
    sent_like = array((peers * TILE, channels), BF16)
    onehot_like = array((rows, groups * pack * slots), BF16)
    places_like = array((slots + peers * TILE, 128), I32)
    weights_like = array(own.shape, BF16)
    picked_like = array((rows, offsets * channels), BF16)
    spread_like = array((groups * pack * slots, channels), BF16)

    def call(kernel, name, args, out_shapes, scratch, flops):
        return pl.pallas_call(
            kernel,
            in_specs=[anywhere] * len(args),
            out_specs=[anywhere] * len(out_shapes),
            out_shape=out_shapes,
            scratch_shapes=[pltpu.VMEM(s.shape, s.dtype) for s in scratch] + [pltpu.SemaphoreType.DMA((12,))],
            compiler_params=pltpu.CompilerParams(vmem_limit_bytes=VMEM_BYTES),
            cost_estimate=pl.CostEstimate(flops=flops, bytes_accessed=10**6, transcendentals=0),
            name=name,
        )(*args)

    def exchange(value):
        return lax.all_to_all(value, "space", 0, 0, tiled=True)

    local_flops = 2 * offsets * rows * channels * (rows + channels)
    payload, = call(
        publish_kernel, "publish", (features, border, wanted), [published_like],
        [block, border, wanted, published_like], 10**8,
    )
    received = exchange(payload)
    total, halo_onehot, places = call(
        functools.partial(first_local_kernel, borders), "first_local", (features, codes, wanted, own, other),
        [total_like, onehot_like, places_like],
        [block, codes, wanted, weights_like, picked_like, total_like, onehot_like, places_like], local_flops,
    )
    latent, normed, send = call(
        encode_kernel, "encode",
        (features, total, received, halo_onehot, places, border, conv_bias, own, other), [block, block, sent_like],
        [block, total_like, published_like, onehot_like, places_like, border, conv_bias, weights_like, spread_like,
         block, block, sent_like], 10**9,
    )
    received = exchange(send)
    total, = call(
        second_local_kernel, "second_local", (normed, codes, own, other), [total_like],
        [block, codes, weights_like, picked_like, total_like], local_flops,
    )
    kept, passed = call(
        functools.partial(decode_kernel, cap), "decode",
        (latent, total, received, halo_onehot, conv_bias, own, other), [array((2, rows, channels), BF16), block],
        [block, total_like, sent_like, onehot_like, conv_bias, weights_like, spread_like, block], 10**9,
    )
    got = lax.ppermute(passed, "phase", swap)
    return lax.dynamic_update_slice(kept, got[None], (1 - phase, 0, 0))[None]


def solution(mesh):
    return jax.shard_map(
        body,
        mesh=mesh,
        in_specs=(
            P(None, "space", None),
            P("phase", None, None, None),
            P(),
            P("space", None),
            P("space", None),
            P("space", None, None),
        ),
        out_specs=P("phase", None, "space", None),
        check_vma=False,
    )
```

```python
import functools

import jax
import jax.numpy as jnp
from jax import lax
from jax.experimental import pallas as pl
from jax.experimental.pallas import tpu as pltpu
from jax.sharding import PartitionSpec as P

BF16 = jnp.bfloat16
F32 = jnp.float32
I32 = jnp.int32
TILE = 8
BLOCK = 128
VMEM_BYTES = 60 * 2**20


def iota(shape, dim):
    return lax.broadcasted_iota(I32, shape, dim)


def onehot(column, width):
    return (column == iota((column.shape[0], width), 1)).astype(BF16)


def dot(a, b):
    return jnp.dot(a, b, preferred_element_type=F32)


def normalise(values):
    mean_square = jnp.mean(values * values, axis=1, keepdims=True)
    return (values * lax.rsqrt(mean_square + 1e-06)).astype(BF16)


def packing(slots, offsets):
    pack = 128 // slots if slots < 128 else 1
    return pack, -(-offsets // pack)


def lookup(column, row):
    shape = (column.shape[0], row.shape[1])
    named = jnp.where(column == iota(shape, 1), jnp.broadcast_to(row.astype(F32), shape), 0.0)
    return jnp.sum(named, axis=1, keepdims=True).astype(I32)


class Copies:
    def __init__(self, sems):
        self.sems = sems
        self.used = 0

    def start(self, source, target):
        copy = pltpu.make_async_copy(source, target, self.sems.at[self.used])
        self.used += 1
        copy.start()
        return copy

    def start_either(self, chosen, copy, other):
        sem = self.sems.at[self.used]
        self.used += 1
        copy, other = (pltpu.make_async_copy(source, target, sem) for source, target in (copy, other))
        pl.when(chosen)(copy.start)
        pl.when(jnp.logical_not(chosen))(other.start)
        return copy


def publish_kernel(
    features_ref, border_ref, wanted_ref, shown_ref, payload_ref, block_ref, border_v, wanted_v, aux_ref, shown_v, sems
):
    copies = Copies(sems)
    loads = [
        copies.start(features_ref.at[lax.axis_index("phase")], block_ref),
        copies.start(border_ref, border_v),
        copies.start(wanted_ref, wanted_v),
    ]
    for load in loads:
        load.wait()
    cap, peers = wanted_v.shape
    place = lookup(iota((border_v.shape[1], 1), 0), border_v[...])
    picked = dot(onehot(place, block_ref.shape[0]), block_ref[...])
    aux_ref[...] = jnp.zeros_like(aux_ref)
    aux_ref[0:cap, 0:peers] = wanted_v[...].astype(F32)
    shown_v[...] = jnp.concatenate([normalise(picked).astype(F32), aux_ref[...]], axis=0).astype(BF16)
    stores = [copies.start(shown_v, shown_ref)]
    for member in range(payload_ref.shape[0]):
        stores.append(copies.start(shown_v, payload_ref.at[member, 0]))
    for store in stores:
        store.wait()


def gather(codes, normed, picked_v, beside=lambda k: None):
    rows, channels = normed.shape
    for k in range(codes.shape[1]):
        picked_v[:, k * channels : (k + 1) * channels] = dot(onehot(codes[:, k : k + 1], rows), normed).astype(BF16)
        beside(k)


def convolved_blocks(picked_v, held_ref):
    rows = picked_v.shape[0]
    matrix = held_ref[...].reshape(picked_v.shape[1], held_ref.shape[2])
    for first in range(0, rows, BLOCK):
        span = pl.ds(first, BLOCK)
        yield span, dot(picked_v[span, :], matrix)


def slot_numbers(rows, per_peer, cap):
    row = iota((rows, 1), 0)
    peer = lax.div(row, per_peer)
    return peer, lax.rem(row - peer * per_peer, cap)


def halo_onehot_group(codes, slots, group, halo_onehot_v):
    rows, offsets = codes.shape
    pack, groups = packing(slots, offsets)
    width = slots * pack
    lane = iota((rows, width), 1)
    named = None
    for j in range(pack):
        k = group * pack + j
        code = codes[:, k : k + 1] + (j * slots - rows) if k < offsets else jnp.full((rows, 1), -1, I32)
        code = jnp.broadcast_to(code, (rows, width))
        named = code if named is None else jnp.where(lane >= j * slots, code, named)
    halo_onehot_v[:, group * width : (group + 1) * width] = (named == lane).astype(BF16)


def published_places(wanted, borders):
    cap, peers = wanted.shape
    half = peers // 2
    upper_here = (lax.axis_index("space") >= half).astype(I32)

    def block_start(peer):
        upper = (peer >= half).astype(I32)
        across = (upper != upper_here).astype(I32)
        return ((peer - half * upper) * 2 + across) * (borders + TILE)

    peer, slot = slot_numbers(peers * cap, cap, cap)
    mine = lax.dot_general(
        onehot(peer, peers), wanted.astype(BF16), (((1,), (1,)), ((), ())), preferred_element_type=F32
    )
    mine = jnp.sum(jnp.where(iota(mine.shape, 1) == slot, mine, 0.0), axis=1, keepdims=True).astype(I32)
    asker, place = slot_numbers(peers * TILE, TILE, cap)
    return jnp.concatenate([block_start(peer) + mine, block_start(asker) + borders + place], axis=0)


def first_local_kernel(
    borders, features_ref, codes_ref, wanted_ref, own_ref, other_ref,
    total_ref, halo_onehot_ref, places_ref,
    block_ref, codes_v, wanted_v, held_ref, picked_v, total_v, halo_onehot_v, places_v, sems,
):
    phase = lax.axis_index("phase")
    copies = Copies(sems)
    loads = [
        copies.start(codes_ref, codes_v),
        copies.start(features_ref.at[phase], block_ref),
        copies.start(wanted_ref, wanted_v),
    ]
    weights_load = copies.start_either(phase == 0, (own_ref, held_ref), (other_ref, held_ref))
    for load in loads:
        load.wait()
    codes = codes_v[...].T
    cap, peers = wanted_v.shape
    slots = peers * cap
    pack, groups = packing(slots, codes.shape[1])
    places_v[...] = jnp.broadcast_to(published_places(wanted_v[...], borders), places_v.shape)

    def beside(k):
        if k % pack == 0:
            halo_onehot_group(codes, slots, k // pack, halo_onehot_v)

    gather(codes, normalise(block_ref[...].astype(F32)), picked_v, beside)
    stores = [copies.start(places_v, places_ref), copies.start(halo_onehot_v, halo_onehot_ref)]
    weights_load.wait()
    for span, term in convolved_blocks(picked_v, held_ref):
        total_v[span, :] = term
        stores.append(copies.start(total_v.at[span], total_ref.at[span]))
    for store in stores:
        store.wait()


def pick_rows(places, source_ref):
    rows = source_ref.shape[0]
    step = next(n for n in range(min(rows, 1536) // 16 * 16, 0, -16) if rows % n == 0)
    found = None
    for first in range(0, rows, step):
        term = dot(onehot(places - first, step), source_ref[first : first + step, :])
        found = term if found is None else found + term
    return found


def spread_halo(halo, held_ref, spread_ref):
    slots, channels = halo.shape
    offsets = held_ref.shape[0]
    whole = spread_ref.shape[0]
    if whole > offsets * slots:
        spread_ref[offsets * slots : whole, :] = jnp.zeros((whole - offsets * slots, channels), BF16)
    for k in range(offsets):
        spread_ref[k * slots : (k + 1) * slots, :] = dot(halo, held_ref[k]).astype(BF16)


def halo_term(halo_onehot_v, span, spread_ref):
    total = None
    for first in range(0, spread_ref.shape[0], 2048):
        lanes = pl.ds(first, min(2048, spread_ref.shape[0] - first))
        term = dot(halo_onehot_v[span, lanes], spread_ref[lanes, :])
        total = term if total is None else total + term
    return total


def residual(values, convolved):
    return (values + jax.nn.silu(convolved)).astype(BF16)


def encode_kernel(
    features_ref, total_ref, received_ref, halo_onehot_ref, places_ref, border_ref, bias_ref, own_ref, other_ref,
    latent_ref, normed_ref, send_ref,
    block_ref, total_v, received_v, halo_onehot_v, places_v, border_v, bias_v, held_ref, spread_ref,
    latent_v, normed_v, send_v, sems,
):
    phase = lax.axis_index("phase")
    copies = Copies(sems)
    early = [
        copies.start(received_ref, received_v),
        copies.start(places_ref, places_v),
        copies.start(border_ref, border_v),
    ]
    weights_load = copies.start_either(phase == 0, (own_ref, held_ref), (other_ref, held_ref))
    late = [
        copies.start(halo_onehot_ref, halo_onehot_v),
        copies.start(total_ref, total_v),
        copies.start(features_ref.at[phase], block_ref),
        copies.start(bias_ref, bias_v),
    ]
    for load in early:
        load.wait()
    slots = places_v.shape[0] - send_v.shape[0]
    found = pick_rows(places_v[:, 0:1], received_v)
    theirs = jnp.where(iota((send_v.shape[0], found.shape[1]), 1) == lax.axis_index("space"), found[slots:], 0.0)
    asked = lookup(jnp.sum(theirs, axis=1, keepdims=True).astype(I32), border_v[...])
    weights_load.wait()
    spread_halo(found[:slots].astype(BF16), held_ref, spread_ref)
    for load in late:
        load.wait()
    term = halo_term(halo_onehot_v, pl.ds(0, block_ref.shape[0]), spread_ref)
    latent = residual(block_ref[...].astype(F32), total_v[...] + term + bias_v[0:1, :])
    latent_v[...] = latent
    stores = [copies.start(latent_v, latent_ref)]
    normed = normalise(latent.astype(F32))
    normed_v[...] = normed
    stores.append(copies.start(normed_v, normed_ref))
    send_v[...] = dot(onehot(asked, normed.shape[0]), normed).astype(BF16)
    stores.append(copies.start(send_v, send_ref))
    for store in stores:
        store.wait()


def second_local_kernel(
    normed_ref, codes_ref, own_ref, other_ref, total_ref, normed_v, codes_v, held_ref, picked_v, total_v, sems
):
    phase = lax.axis_index("phase")
    copies = Copies(sems)
    early = [copies.start(codes_ref, codes_v), copies.start(normed_ref, normed_v)]
    weights_load = copies.start_either(phase == 1, (own_ref, held_ref), (other_ref, held_ref))
    for load in early:
        load.wait()
    gather(codes_v[...].T, normed_v[...], picked_v)
    weights_load.wait()
    stores = []
    for span, term in convolved_blocks(picked_v, held_ref):
        total_v[span, :] = term
        stores.append(copies.start(total_v.at[span], total_ref.at[span]))
    for store in stores:
        store.wait()


def decode_kernel(
    cap, latent_ref, total_ref, received_ref, halo_onehot_ref, bias_ref, own_ref, other_ref, kept_ref, passed_ref,
    latent_v, total_v, received_v, halo_onehot_v, bias_v, held_ref, spread_ref, recon_v, sems,
):
    first = lax.axis_index("phase") == 0
    copies = Copies(sems)
    received_load = copies.start(received_ref, received_v)
    weights_load = copies.start_either(first, (other_ref, held_ref), (own_ref, held_ref))
    late = [
        copies.start(halo_onehot_ref, halo_onehot_v),
        copies.start(total_ref, total_v),
        copies.start(latent_ref, latent_v),
        copies.start(bias_ref, bias_v),
    ]
    received_load.wait()
    peer, slot = slot_numbers(received_v.shape[0] // TILE * cap, cap, cap)
    halo = pick_rows(peer * TILE + slot, received_v).astype(BF16)
    weights_load.wait()
    spread_halo(halo, held_ref, spread_ref)
    for load in late:
        load.wait()
    stores = [copies.start_either(first, (latent_v, kept_ref.at[0]), (latent_v, passed_ref))]
    term = halo_term(halo_onehot_v, pl.ds(0, latent_v.shape[0]), spread_ref)
    recon_v[...] = residual(latent_v[...].astype(F32), total_v[...] + term + bias_v[1:2, :])
    stores.append(copies.start_either(first, (recon_v, passed_ref), (recon_v, kept_ref.at[1])))
    for store in stores:
        store.wait()


def body(features, weights, conv_bias, rulebook, border, pull_slots):
    micro, rows, channels = features.shape
    peers, cap = pull_slots.shape[1:]
    borders = border.shape[1]
    offsets = rulebook.shape[1]
    slots = peers * cap
    half = peers // 2
    pack, groups = packing(slots, offsets)
    published = peers * (borders + TILE)
    phase = lax.axis_index("phase")
    wanted = pull_slots[0].T
    codes = rulebook.T
    own = weights[0]
    swap = [(0, 1), (1, 0)]
    other = lax.ppermute(own, "phase", swap)

    anywhere = pl.BlockSpec(memory_space=pl.ANY)
    array = jax.ShapeDtypeStruct
    block = array((rows, channels), BF16)
    total_like = array((rows, channels), F32)
    published_like = array((published, channels), BF16)
    shown_like = array((borders + TILE, channels), BF16)
    sent_like = array((peers * TILE, channels), BF16)
    onehot_like = array((rows, groups * pack * slots), BF16)
    places_like = array((slots + peers * TILE, 128), I32)
    weights_like = array(own.shape, BF16)
    picked_like = array((rows, offsets * channels), BF16)
    spread_like = array((groups * pack * slots, channels), BF16)

    def call(kernel, name, args, out_shapes, scratch, flops):
        return pl.pallas_call(
            kernel,
            in_specs=[anywhere] * len(args),
            out_specs=[anywhere] * len(out_shapes),
            out_shape=out_shapes,
            scratch_shapes=[pltpu.VMEM(s.shape, s.dtype) for s in scratch] + [pltpu.SemaphoreType.DMA((max(12, half + 4),))],
            compiler_params=pltpu.CompilerParams(vmem_limit_bytes=VMEM_BYTES),
            cost_estimate=pl.CostEstimate(flops=flops, bytes_accessed=10**6, transcendentals=0),
            name=name,
        )(*args)

    def exchange(value, groups=None):
        return lax.all_to_all(value, "space", 0, 0, tiled=True, axis_index_groups=groups)

    local_flops = 2 * offsets * rows * channels * (rows + channels)
    shown, payload = call(
        publish_kernel, "publish", (features, border, wanted), [shown_like, array((half, 2, *shown_like.shape), BF16)],
        [block, border, wanted, array((TILE, channels), F32), shown_like], 10**8,
    )
    across = lax.ppermute(shown, "space", [(place, (place + half) % peers) for place in range(peers)])
    payload = lax.dynamic_update_slice(
        payload, jnp.broadcast_to(across, (half, 1, *across.shape)), (0, 1, 0, 0)
    ).reshape(published, channels)
    payload, other = lax.optimization_barrier((payload, other))
    received = exchange(payload, [list(range(half)), list(range(half, peers))])
    total, halo_onehot, places = call(
        functools.partial(first_local_kernel, borders), "first_local", (features, codes, wanted, own, other),
        [total_like, onehot_like, places_like],
        [block, codes, wanted, weights_like, picked_like, total_like, onehot_like, places_like], local_flops,
    )
    latent, normed, send = call(
        encode_kernel, "encode",
        (features, total, received, halo_onehot, places, border, conv_bias, own, other), [block, block, sent_like],
        [block, total_like, published_like, onehot_like, places_like, border, conv_bias, weights_like, spread_like,
         block, block, sent_like], 10**9,
    )
    received = exchange(send)
    total, = call(
        second_local_kernel, "second_local", (normed, codes, own, other), [total_like],
        [block, codes, weights_like, picked_like, total_like], local_flops,
    )
    kept, passed = call(
        functools.partial(decode_kernel, cap), "decode",
        (latent, total, received, halo_onehot, conv_bias, own, other), [array((2, rows, channels), BF16), block],
        [block, total_like, sent_like, onehot_like, conv_bias, weights_like, spread_like, block], 10**9,
    )
    got = lax.ppermute(passed, "phase", swap)
    return lax.dynamic_update_slice(kept, got[None], (1 - phase, 0, 0))[None]


def solution(mesh):
    return jax.shard_map(
        body,
        mesh=mesh,
        in_specs=(
            P(None, "space", None),
            P("phase", None, None, None),
            P(),
            P("space", None),
            P("space", None),
            P("space", None, None),
        ),
        out_specs=P("phase", None, "space", None),
        check_vma=False,
    )
```

```python
import functools

import jax
import jax.numpy as jnp
from jax import lax
from jax.experimental import pallas as pl
from jax.experimental.pallas import tpu as pltpu
from jax.sharding import PartitionSpec as P

BF16 = jnp.bfloat16
F32 = jnp.float32
I32 = jnp.int32
TILE = 8
BLOCK = 128
VMEM_BYTES = 60 * 2**20
DECODE_BYTES = 50 * 2**20
PADDED_ROWS = 15 * 1024


def iota(shape, dim):
    return lax.broadcasted_iota(I32, shape, dim)


def onehot(column, width):
    return (column == iota((column.shape[0], width), 1)).astype(BF16)


def dot(a, b):
    return jnp.dot(a, b, preferred_element_type=F32)


def normalise(values):
    mean_square = jnp.mean(values * values, axis=1, keepdims=True)
    return (values * lax.rsqrt(mean_square + 1e-06)).astype(BF16)


def packing(slots, offsets):
    pack = 128 // slots if slots < 128 else 1
    return pack, -(-offsets // pack)


def lookup(column, row):
    shape = (column.shape[0], row.shape[1])
    named = jnp.where(column == iota(shape, 1), jnp.broadcast_to(row.astype(F32), shape), 0.0)
    return jnp.sum(named, axis=1, keepdims=True).astype(I32)


class Copies:
    def __init__(self, sems):
        self.sems = sems
        self.used = 0

    def start(self, source, target):
        copy = pltpu.make_async_copy(source, target, self.sems.at[self.used])
        self.used += 1
        copy.start()
        return copy

    def start_either(self, chosen, copy, other):
        sem = self.sems.at[self.used]
        self.used += 1
        copy, other = (pltpu.make_async_copy(source, target, sem) for source, target in (copy, other))
        pl.when(chosen)(copy.start)
        pl.when(jnp.logical_not(chosen))(other.start)
        return copy


def publish_kernel(
    features_ref, border_ref, wanted_ref, shown_ref, payload_ref, block_ref, border_v, wanted_v, aux_ref, shown_v, sems
):
    copies = Copies(sems)
    loads = [
        copies.start(features_ref.at[lax.axis_index("phase")], block_ref),
        copies.start(border_ref, border_v),
        copies.start(wanted_ref, wanted_v),
    ]
    for load in loads:
        load.wait()
    cap, peers = wanted_v.shape
    place = lookup(iota((border_v.shape[1], 1), 0), border_v[...])
    picked = dot(onehot(place, block_ref.shape[0]), block_ref[...])
    aux_ref[...] = jnp.zeros_like(aux_ref)
    aux_ref[0:cap, 0:peers] = wanted_v[...].astype(F32)
    shown_v[...] = jnp.concatenate([normalise(picked).astype(F32), aux_ref[...]], axis=0).astype(BF16)
    stores = [copies.start(shown_v, shown_ref)]
    for member in range(payload_ref.shape[0]):
        stores.append(copies.start(shown_v, payload_ref.at[member, 0]))
    for store in stores:
        store.wait()


def gather(codes, normed, picked_v, beside=lambda k: None):
    rows, channels = normed.shape
    offsets = codes.shape[1]
    for k in range(offsets):
        if k == offsets // 2:
            picked_v[:, k * channels : (k + 1) * channels] = normed
        else:
            picked_v[:, k * channels : (k + 1) * channels] = dot(onehot(codes[:, k : k + 1], rows), normed).astype(BF16)
        beside(k)


def convolved_blocks(picked_v, held_ref):
    rows = picked_v.shape[0]
    matrix = held_ref[...].reshape(picked_v.shape[1], held_ref.shape[2])
    for first in range(0, rows, BLOCK):
        span = pl.ds(first, BLOCK)
        yield span, dot(picked_v[span, :], matrix)


def slot_numbers(rows, per_peer, cap):
    row = iota((rows, 1), 0)
    peer = lax.div(row, per_peer)
    return peer, lax.rem(row - peer * per_peer, cap)


def halo_onehot_group(codes, slots, group, halo_onehot_v):
    rows, offsets = codes.shape
    pack, groups = packing(slots, offsets)
    width = slots * pack
    lane = iota((rows, width), 1)
    named = None
    for j in range(pack):
        k = group * pack + j
        code = codes[:, k : k + 1] + (j * slots - rows) if k < offsets else jnp.full((rows, 1), -1, I32)
        code = jnp.broadcast_to(code, (rows, width))
        named = code if named is None else jnp.where(lane >= j * slots, code, named)
    halo_onehot_v[:, group * width : (group + 1) * width] = (named == lane).astype(BF16)


def published_places(wanted, borders):
    cap, peers = wanted.shape
    half = peers // 2
    upper_here = (lax.axis_index("space") >= half).astype(I32)

    def block_start(peer):
        upper = (peer >= half).astype(I32)
        across = (upper != upper_here).astype(I32)
        return ((peer - half * upper) * 2 + across) * (borders + TILE)

    peer, slot = slot_numbers(peers * cap, cap, cap)
    mine = lax.dot_general(
        onehot(peer, peers), wanted.astype(BF16), (((1,), (1,)), ((), ())), preferred_element_type=F32
    )
    mine = jnp.sum(jnp.where(iota(mine.shape, 1) == slot, mine, 0.0), axis=1, keepdims=True).astype(I32)
    asker, place = slot_numbers(peers * TILE, TILE, cap)
    return jnp.concatenate([block_start(peer) + mine, block_start(asker) + borders + place], axis=0)


def first_local_kernel(
    borders, features_ref, codes_ref, wanted_ref, own_ref, other_ref,
    total_ref, halo_onehot_ref, places_ref, columns_ref,
    block_ref, codes_v, wanted_v, held_ref, picked_v, total_v, halo_onehot_v, places_v, columns_v, sems,
):
    phase = lax.axis_index("phase")
    copies = Copies(sems)
    loads = [
        copies.start(codes_ref, codes_v),
        copies.start(features_ref.at[phase], block_ref),
        copies.start(wanted_ref, wanted_v),
    ]
    weights_load = copies.start_either(phase == 0, (own_ref, held_ref), (other_ref, held_ref))
    for load in loads:
        load.wait()
    codes = codes_v[...].T
    columns_v[:, 0 : codes.shape[1]] = codes
    cap, peers = wanted_v.shape
    slots = peers * cap
    pack, groups = packing(slots, codes.shape[1])
    places_v[...] = jnp.broadcast_to(published_places(wanted_v[...], borders), places_v.shape)

    def beside(k):
        if k % pack == 0:
            halo_onehot_group(codes, slots, k // pack, halo_onehot_v)

    gather(codes, normalise(block_ref[...].astype(F32)), picked_v, beside)
    stores = [copies.start(places_v, places_ref), copies.start(columns_v, columns_ref), copies.start(halo_onehot_v, halo_onehot_ref)]
    weights_load.wait()
    for span, term in convolved_blocks(picked_v, held_ref):
        total_v[span, :] = term
        stores.append(copies.start(total_v.at[span], total_ref.at[span]))
    for store in stores:
        store.wait()


def pick_rows(places, source_ref):
    rows = source_ref.shape[0]
    step = next(n for n in range(min(rows, 1536) // 16 * 16, 0, -16) if rows % n == 0)
    found = None
    for first in range(0, rows, step):
        term = dot(onehot(places - first, step), source_ref[first : first + step, :])
        found = term if found is None else found + term
    return found


def spread_halo(halo, held_ref, spread_ref):
    slots, channels = halo.shape
    offsets = held_ref.shape[0]
    whole = spread_ref.shape[0]
    if whole > offsets * slots:
        spread_ref[offsets * slots : whole, :] = jnp.zeros((whole - offsets * slots, channels), BF16)
    for k in range(offsets):
        spread_ref[k * slots : (k + 1) * slots, :] = dot(halo, held_ref[k]).astype(BF16)


def halo_term(halo_onehot_v, span, spread_ref):
    total = None
    for first in range(0, spread_ref.shape[0], 2048):
        lanes = pl.ds(first, min(2048, spread_ref.shape[0] - first))
        term = dot(halo_onehot_v[span, lanes], spread_ref[lanes, :])
        total = term if total is None else total + term
    return total


def residual(values, convolved):
    return (values + jax.nn.silu(convolved)).astype(BF16)


def encode_kernel(
    features_ref, total_ref, received_ref, halo_onehot_ref, places_ref, border_ref, bias_ref, own_ref, other_ref,
    latent_ref, normed_ref, send_ref,
    block_ref, total_v, received_v, halo_onehot_v, places_v, border_v, bias_v, held_ref, spread_ref,
    latent_v, normed_v, send_v, sems,
):
    phase = lax.axis_index("phase")
    copies = Copies(sems)
    early = [
        copies.start(received_ref, received_v),
        copies.start(places_ref, places_v),
        copies.start(border_ref, border_v),
    ]
    weights_load = copies.start_either(phase == 0, (own_ref, held_ref), (other_ref, held_ref))
    late = [
        copies.start(halo_onehot_ref, halo_onehot_v),
        copies.start(total_ref, total_v),
        copies.start(features_ref.at[phase], block_ref),
        copies.start(bias_ref, bias_v),
    ]
    for load in early:
        load.wait()
    slots = places_v.shape[0] - send_v.shape[0]
    found = pick_rows(places_v[:, 0:1], received_v)
    theirs = jnp.where(iota((send_v.shape[0], found.shape[1]), 1) == lax.axis_index("space"), found[slots:], 0.0)
    asked = lookup(jnp.sum(theirs, axis=1, keepdims=True).astype(I32), border_v[...])
    weights_load.wait()
    spread_halo(found[:slots].astype(BF16), held_ref, spread_ref)
    for load in late:
        load.wait()
    term = halo_term(halo_onehot_v, pl.ds(0, block_ref.shape[0]), spread_ref)
    latent = residual(block_ref[...].astype(F32), total_v[...] + term + bias_v[0:1, :])
    latent_v[...] = latent
    stores = [copies.start(latent_v, latent_ref)]
    normed = normalise(latent.astype(F32))
    normed_v[...] = normed
    stores.append(copies.start(normed_v, normed_ref))
    send_v[...] = dot(onehot(asked, normed.shape[0]), normed).astype(BF16)
    stores.append(copies.start(send_v, send_ref))
    for store in stores:
        store.wait()


def second_local_kernel(
    normed_ref, codes_ref, own_ref, other_ref, total_ref, normed_v, codes_v, held_ref, picked_v, total_v, sems
):
    phase = lax.axis_index("phase")
    copies = Copies(sems)
    early = [copies.start(codes_ref, codes_v), copies.start(normed_ref, normed_v)]
    weights_load = copies.start_either(phase == 1, (own_ref, held_ref), (other_ref, held_ref))
    for load in early:
        load.wait()
    gather(codes_v[:, 0 : picked_v.shape[1] // normed_v.shape[1]], normed_v[...], picked_v)
    weights_load.wait()
    stores = []
    for span, term in convolved_blocks(picked_v, held_ref):
        total_v[span, :] = term
        stores.append(copies.start(total_v.at[span], total_ref.at[span]))
    for store in stores:
        store.wait()


def decode_kernel(
    cap, latent_ref, total_ref, received_ref, halo_onehot_ref, bias_ref, own_ref, other_ref, kept_ref, passed_ref,
    latent_v, total_v, received_v, halo_onehot_v, bias_v, held_ref, spread_ref, recon_v, sems,
):
    first = lax.axis_index("phase") == 0
    copies = Copies(sems)
    received_load = copies.start(received_ref, received_v)
    weights_load = copies.start_either(first, (other_ref, held_ref), (own_ref, held_ref))
    late = [
        copies.start(halo_onehot_ref, halo_onehot_v),
        copies.start(total_ref.at[pl.ds(0, total_v.shape[0])], total_v),
        copies.start(latent_ref, latent_v),
        copies.start(bias_ref, bias_v),
    ]
    received_load.wait()
    peer, slot = slot_numbers(received_v.shape[0] // TILE * cap, cap, cap)
    halo = pick_rows(peer * TILE + slot, received_v).astype(BF16)
    weights_load.wait()
    spread_halo(halo, held_ref, spread_ref)
    for load in late:
        load.wait()
    stores = [copies.start_either(first, (latent_v, kept_ref.at[0]), (latent_v, passed_ref))]
    term = halo_term(halo_onehot_v, pl.ds(0, latent_v.shape[0]), spread_ref)
    recon_v[...] = residual(latent_v[...].astype(F32), total_v[...] + term + bias_v[1:2, :])
    stores.append(copies.start_either(first, (recon_v, passed_ref), (recon_v, kept_ref.at[1])))
    for store in stores:
        store.wait()


def body(features, weights, conv_bias, rulebook, border, pull_slots):
    micro, rows, channels = features.shape
    peers, cap = pull_slots.shape[1:]
    borders = border.shape[1]
    offsets = rulebook.shape[1]
    slots = peers * cap
    half = peers // 2
    pack, groups = packing(slots, offsets)
    published = peers * (borders + TILE)
    phase = lax.axis_index("phase")
    wanted = pull_slots[0].T
    codes = rulebook.T
    own = weights[0]
    swap = [(0, 1), (1, 0)]
    other = lax.ppermute(own, "phase", swap)

    anywhere = pl.BlockSpec(memory_space=pl.ANY)
    array = jax.ShapeDtypeStruct
    block = array((rows, channels), BF16)
    total_like = array((rows, channels), F32)
    published_like = array((published, channels), BF16)
    shown_like = array((borders + TILE, channels), BF16)
    sent_like = array((peers * TILE, channels), BF16)
    onehot_like = array((rows, groups * pack * slots), BF16)
    places_like = array((slots + peers * TILE, 128), I32)
    columns_like = array((rows, -(-offsets // 128) * 128), I32)
    weights_like = array(own.shape, BF16)
    picked_like = array((rows, offsets * channels), BF16)
    spread_like = array((groups * pack * slots, channels), BF16)

    def call(kernel, name, args, out_shapes, scratch, flops, limit=VMEM_BYTES):
        return pl.pallas_call(
            kernel,
            in_specs=[anywhere] * len(args),
            out_specs=[anywhere] * len(out_shapes),
            out_shape=out_shapes,
            scratch_shapes=[pltpu.VMEM(s.shape, s.dtype) for s in scratch] + [pltpu.SemaphoreType.DMA((max(12, half + 4),))],
            compiler_params=pltpu.CompilerParams(vmem_limit_bytes=limit),
            cost_estimate=pl.CostEstimate(flops=flops, bytes_accessed=10**6, transcendentals=0),
            name=name,
        )(*args)

    def exchange(value, groups=None):
        return lax.all_to_all(value, "space", 0, 0, tiled=True, axis_index_groups=groups)

    local_flops = 2 * offsets * rows * channels * (rows + channels)
    shown, payload = call(
        publish_kernel, "publish", (features, border, wanted), [shown_like, array((half, 2, *shown_like.shape), BF16)],
        [block, border, wanted, array((TILE, channels), F32), shown_like], 10**8,
    )
    across = lax.ppermute(shown, "space", [(place, (place + half) % peers) for place in range(peers)])
    payload = lax.dynamic_update_slice(
        payload, jnp.broadcast_to(across, (half, 1, *across.shape)), (0, 1, 0, 0)
    ).reshape(published, channels)
    payload, other = lax.optimization_barrier((payload, other))
    received = exchange(payload, [list(range(half)), list(range(half, peers))])
    total, halo_onehot, places, columns = call(
        functools.partial(first_local_kernel, borders), "first_local", (features, codes, wanted, own, other),
        [total_like, onehot_like, places_like, columns_like],
        [block, codes, wanted, weights_like, picked_like, total_like, onehot_like, places_like, columns_like], local_flops,
    )
    latent, normed, send = call(
        encode_kernel, "encode",
        (features, total, received, halo_onehot, places, border, conv_bias, own, other), [block, block, sent_like],
        [block, total_like, published_like, onehot_like, places_like, border, conv_bias, weights_like, spread_like,
         block, block, sent_like], 10**9,
    )
    received = exchange(send)
    total, = call(
        second_local_kernel, "second_local", (normed, columns, own, other), [array((max(rows, PADDED_ROWS), channels), F32)],
        [block, columns_like, weights_like, picked_like, total_like], local_flops,
    )
    kept, passed = call(
        functools.partial(decode_kernel, cap), "decode",
        (latent, total, received, halo_onehot, conv_bias, own, other), [array((2, rows, channels), BF16), block],
        [block, total_like, sent_like, onehot_like, conv_bias, weights_like, spread_like, block], 10**9, DECODE_BYTES,
    )
    got = lax.ppermute(passed, "phase", swap)
    return lax.dynamic_update_slice(kept, got[None], (1 - phase, 0, 0))[None]


def solution(mesh):
    return jax.shard_map(
        body,
        mesh=mesh,
        in_specs=(
            P(None, "space", None),
            P("phase", None, None, None),
            P(),
            P("space", None),
            P("space", None),
            P("space", None, None),
        ),
        out_specs=P("phase", None, "space", None),
        check_vma=False,
    )
```

```python
import functools

import jax
import jax.numpy as jnp
from jax import lax
from jax.experimental import pallas as pl
from jax.experimental.pallas import tpu as pltpu
from jax.sharding import PartitionSpec as P

BF16 = jnp.bfloat16
F32 = jnp.float32
I32 = jnp.int32
TILE = 8
BLOCK = 128
CHUNK = 9
VMEM_BYTES = 60 * 2**20
DECODE_BYTES = 50 * 2**20
PADDED_ROWS = 15 * 1024


def iota(shape, dim):
    return lax.broadcasted_iota(I32, shape, dim)


def onehot(column, width):
    return (column == iota((column.shape[0], width), 1)).astype(BF16)


def dot(a, b):
    return jnp.dot(a, b, preferred_element_type=F32)


def normalise(values):
    mean_square = jnp.mean(values * values, axis=1, keepdims=True)
    return (values * lax.rsqrt(mean_square + 1e-06)).astype(BF16)


def packing(slots, offsets):
    pack = 128 // slots if slots < 128 else 1
    return pack, -(-offsets // pack)


def lookup(column, row):
    shape = (column.shape[0], row.shape[1])
    named = jnp.where(column == iota(shape, 1), jnp.broadcast_to(row.astype(F32), shape), 0.0)
    return jnp.sum(named, axis=1, keepdims=True).astype(I32)


class Copies:
    def __init__(self, sems):
        self.sems = sems
        self.used = 0

    def start(self, source, target):
        copy = pltpu.make_async_copy(source, target, self.sems.at[self.used])
        self.used += 1
        copy.start()
        return copy

    def start_chunks(self, chosen, source, other, target, step):
        count = target.shape[0]
        spans = [pl.ds(first, min(step, count - first)) for first in range(0, count, step)]
        return [self.start_either(chosen, (source.at[s], target.at[s]), (other.at[s], target.at[s])) for s in spans]

    def start_either(self, chosen, copy, other):
        sem = self.sems.at[self.used]
        self.used += 1
        copy, other = (pltpu.make_async_copy(source, target, sem) for source, target in (copy, other))
        pl.when(chosen)(copy.start)
        pl.when(jnp.logical_not(chosen))(other.start)
        return copy


def publish_kernel(
    features_ref, border_ref, wanted_ref, shown_ref, payload_ref, block_ref, border_v, wanted_v, aux_ref, shown_v, sems
):
    copies = Copies(sems)
    loads = [
        copies.start(features_ref.at[lax.axis_index("phase")], block_ref),
        copies.start(border_ref, border_v),
        copies.start(wanted_ref, wanted_v),
    ]
    for load in loads:
        load.wait()
    cap, peers = wanted_v.shape
    place = lookup(iota((border_v.shape[1], 1), 0), border_v[...])
    picked = dot(onehot(place, block_ref.shape[0]), block_ref[...])
    aux_ref[...] = jnp.zeros_like(aux_ref)
    aux_ref[0:cap, 0:peers] = wanted_v[...].astype(F32)
    shown_v[...] = jnp.concatenate([normalise(picked).astype(F32), aux_ref[...]], axis=0).astype(BF16)
    stores = [copies.start(shown_v, shown_ref)]
    for member in range(payload_ref.shape[0]):
        stores.append(copies.start(shown_v, payload_ref.at[member, 0]))
    for store in stores:
        store.wait()


def gather(codes, normed, picked_v, beside=lambda k: None):
    rows, channels = normed.shape
    offsets = codes.shape[1]
    for k in range(offsets):
        if k == offsets // 2:
            picked_v[:, k * channels : (k + 1) * channels] = normed
        else:
            picked_v[:, k * channels : (k + 1) * channels] = dot(onehot(codes[:, k : k + 1], rows), normed).astype(BF16)
        beside(k)


def convolved_blocks(picked_v, held_ref):
    rows = picked_v.shape[0]
    matrix = held_ref[...].reshape(picked_v.shape[1], held_ref.shape[2])
    for first in range(0, rows, BLOCK):
        span = pl.ds(first, BLOCK)
        yield span, dot(picked_v[span, :], matrix)


def slot_numbers(rows, per_peer, cap):
    row = iota((rows, 1), 0)
    peer = lax.div(row, per_peer)
    return peer, lax.rem(row - peer * per_peer, cap)


def halo_onehot_group(codes, slots, group, halo_onehot_v):
    rows, offsets = codes.shape
    pack, groups = packing(slots, offsets)
    width = slots * pack
    lane = iota((rows, width), 1)
    named = None
    for j in range(pack):
        k = group * pack + j
        code = codes[:, k : k + 1] + (j * slots - rows) if k < offsets else jnp.full((rows, 1), -1, I32)
        code = jnp.broadcast_to(code, (rows, width))
        named = code if named is None else jnp.where(lane >= j * slots, code, named)
    halo_onehot_v[:, group * width : (group + 1) * width] = (named == lane).astype(BF16)


def published_places(wanted, borders):
    cap, peers = wanted.shape
    half = peers // 2
    upper_here = (lax.axis_index("space") >= half).astype(I32)

    def block_start(peer):
        upper = (peer >= half).astype(I32)
        across = (upper != upper_here).astype(I32)
        return ((peer - half * upper) * 2 + across) * (borders + TILE)

    peer, slot = slot_numbers(peers * cap, cap, cap)
    mine = lax.dot_general(
        onehot(peer, peers), wanted.astype(BF16), (((1,), (1,)), ((), ())), preferred_element_type=F32
    )
    mine = jnp.sum(jnp.where(iota(mine.shape, 1) == slot, mine, 0.0), axis=1, keepdims=True).astype(I32)
    asker, place = slot_numbers(peers * TILE, TILE, cap)
    return jnp.concatenate([block_start(peer) + mine, block_start(asker) + borders + place], axis=0)


def first_local_kernel(
    borders, features_ref, codes_ref, wanted_ref, own_ref, other_ref,
    total_ref, halo_onehot_ref, places_ref, columns_ref,
    block_ref, codes_v, wanted_v, held_ref, picked_v, total_v, halo_onehot_v, places_v, columns_v, sems,
):
    phase = lax.axis_index("phase")
    copies = Copies(sems)
    loads = [
        copies.start(codes_ref, codes_v),
        copies.start(features_ref.at[phase], block_ref),
        copies.start(wanted_ref, wanted_v),
    ]
    weights_load = copies.start_either(phase == 0, (own_ref, held_ref), (other_ref, held_ref))
    for load in loads:
        load.wait()
    codes = codes_v[...].T
    columns_v[:, 0 : codes.shape[1]] = codes
    cap, peers = wanted_v.shape
    slots = peers * cap
    pack, groups = packing(slots, codes.shape[1])
    places_v[...] = jnp.broadcast_to(published_places(wanted_v[...], borders), places_v.shape)

    def beside(k):
        if k % pack == 0:
            halo_onehot_group(codes, slots, k // pack, halo_onehot_v)

    gather(codes, normalise(block_ref[...].astype(F32)), picked_v, beside)
    stores = [copies.start(places_v, places_ref), copies.start(columns_v, columns_ref), copies.start(halo_onehot_v, halo_onehot_ref)]
    weights_load.wait()
    for span, term in convolved_blocks(picked_v, held_ref):
        total_v[span, :] = term
        stores.append(copies.start(total_v.at[span], total_ref.at[span]))
    for store in stores:
        store.wait()


def pick_rows(places, source_ref):
    rows = source_ref.shape[0]
    step = next(n for n in range(min(rows, 1536) // 16 * 16, 0, -16) if rows % n == 0)
    found = None
    for first in range(0, rows, step):
        term = dot(onehot(places - first, step), source_ref[first : first + step, :])
        found = term if found is None else found + term
    return found


def spread_halo(halo, loads, held_ref, spread_ref):
    slots, channels = halo.shape
    offsets = held_ref.shape[0]
    whole = spread_ref.shape[0]
    if whole > offsets * slots:
        spread_ref[offsets * slots : whole, :] = jnp.zeros((whole - offsets * slots, channels), BF16)
    step = -(-offsets // len(loads))
    for at, load in enumerate(loads):
        load.wait()
        for k in range(at * step, min((at + 1) * step, offsets)):
            spread_ref[k * slots : (k + 1) * slots, :] = dot(halo, held_ref[k]).astype(BF16)


def halo_term(halo_onehot_v, span, spread_ref):
    total = None
    for first in range(0, spread_ref.shape[0], 2048):
        lanes = pl.ds(first, min(2048, spread_ref.shape[0] - first))
        term = dot(halo_onehot_v[span, lanes], spread_ref[lanes, :])
        total = term if total is None else total + term
    return total


def residual(values, convolved):
    return (values + jax.nn.silu(convolved)).astype(BF16)


def encode_kernel(
    features_ref, total_ref, received_ref, halo_onehot_ref, places_ref, border_ref, bias_ref, own_ref, other_ref,
    latent_ref, normed_ref, send_ref,
    block_ref, total_v, received_v, halo_onehot_v, places_v, border_v, bias_v, held_ref, spread_ref,
    latent_v, normed_v, send_v, sems,
):
    phase = lax.axis_index("phase")
    copies = Copies(sems)
    early = [
        copies.start(received_ref, received_v),
        copies.start(places_ref, places_v),
        copies.start(border_ref, border_v),
    ]
    weights_load = copies.start_either(phase == 0, (own_ref, held_ref), (other_ref, held_ref))
    late = [
        copies.start(halo_onehot_ref, halo_onehot_v),
        copies.start(total_ref, total_v),
        copies.start(features_ref.at[phase], block_ref),
        copies.start(bias_ref, bias_v),
    ]
    for load in early:
        load.wait()
    slots = places_v.shape[0] - send_v.shape[0]
    found = pick_rows(places_v[:, 0:1], received_v)
    theirs = jnp.where(iota((send_v.shape[0], found.shape[1]), 1) == lax.axis_index("space"), found[slots:], 0.0)
    asked = lookup(jnp.sum(theirs, axis=1, keepdims=True).astype(I32), border_v[...])
    spread_halo(found[:slots].astype(BF16), [weights_load], held_ref, spread_ref)
    for load in late:
        load.wait()
    term = halo_term(halo_onehot_v, pl.ds(0, block_ref.shape[0]), spread_ref)
    latent = residual(block_ref[...].astype(F32), total_v[...] + term + bias_v[0:1, :])
    latent_v[...] = latent
    stores = [copies.start(latent_v, latent_ref)]
    normed = normalise(latent.astype(F32))
    normed_v[...] = normed
    stores.append(copies.start(normed_v, normed_ref))
    send_v[...] = dot(onehot(asked, normed.shape[0]), normed).astype(BF16)
    stores.append(copies.start(send_v, send_ref))
    for store in stores:
        store.wait()


def second_local_kernel(
    normed_ref, codes_ref, own_ref, other_ref, total_ref, normed_v, codes_v, held_ref, picked_v, total_v, sems
):
    phase = lax.axis_index("phase")
    copies = Copies(sems)
    early = [copies.start(codes_ref, codes_v), copies.start(normed_ref, normed_v)]
    weights_load = copies.start_either(phase == 1, (own_ref, held_ref), (other_ref, held_ref))
    for load in early:
        load.wait()
    gather(codes_v[:, 0 : picked_v.shape[1] // normed_v.shape[1]], normed_v[...], picked_v)
    weights_load.wait()
    stores = []
    for span, term in convolved_blocks(picked_v, held_ref):
        total_v[span, :] = term
        stores.append(copies.start(total_v.at[span], total_ref.at[span]))
    for store in stores:
        store.wait()


def decode_kernel(
    cap, latent_ref, total_ref, received_ref, halo_onehot_ref, bias_ref, own_ref, other_ref, kept_ref, passed_ref,
    latent_v, total_v, received_v, halo_onehot_v, bias_v, held_ref, spread_ref, recon_v, sems,
):
    first = lax.axis_index("phase") == 0
    copies = Copies(sems)
    received_load = copies.start(received_ref, received_v)
    weights_loads = copies.start_chunks(first, other_ref, own_ref, held_ref, CHUNK)
    late = [
        copies.start(halo_onehot_ref, halo_onehot_v),
        copies.start(total_ref.at[pl.ds(0, total_v.shape[0])], total_v),
        copies.start(latent_ref, latent_v),
        copies.start(bias_ref, bias_v),
    ]
    received_load.wait()
    peer, slot = slot_numbers(received_v.shape[0] // TILE * cap, cap, cap)
    halo = pick_rows(peer * TILE + slot, received_v).astype(BF16)
    spread_halo(halo, weights_loads, held_ref, spread_ref)
    for load in late:
        load.wait()
    stores = [copies.start_either(first, (latent_v, kept_ref.at[0]), (latent_v, passed_ref))]
    term = halo_term(halo_onehot_v, pl.ds(0, latent_v.shape[0]), spread_ref)
    recon_v[...] = residual(latent_v[...].astype(F32), total_v[...] + term + bias_v[1:2, :])
    stores.append(copies.start_either(first, (recon_v, passed_ref), (recon_v, kept_ref.at[1])))
    for store in stores:
        store.wait()


def body(features, weights, conv_bias, rulebook, border, pull_slots):
    micro, rows, channels = features.shape
    peers, cap = pull_slots.shape[1:]
    borders = border.shape[1]
    offsets = rulebook.shape[1]
    slots = peers * cap
    half = peers // 2
    pack, groups = packing(slots, offsets)
    published = peers * (borders + TILE)
    phase = lax.axis_index("phase")
    wanted = pull_slots[0].T
    codes = rulebook.T
    own = weights[0]
    swap = [(0, 1), (1, 0)]
    other = lax.ppermute(own, "phase", swap)

    anywhere = pl.BlockSpec(memory_space=pl.ANY)
    array = jax.ShapeDtypeStruct
    block = array((rows, channels), BF16)
    total_like = array((rows, channels), F32)
    published_like = array((published, channels), BF16)
    shown_like = array((borders + TILE, channels), BF16)
    sent_like = array((peers * TILE, channels), BF16)
    onehot_like = array((rows, groups * pack * slots), BF16)
    places_like = array((slots + peers * TILE, 128), I32)
    columns_like = array((rows, -(-offsets // 128) * 128), I32)
    weights_like = array(own.shape, BF16)
    picked_like = array((rows, offsets * channels), BF16)
    spread_like = array((groups * pack * slots, channels), BF16)

    def call(kernel, name, args, out_shapes, scratch, flops, limit=VMEM_BYTES):
        return pl.pallas_call(
            kernel,
            in_specs=[anywhere] * len(args),
            out_specs=[anywhere] * len(out_shapes),
            out_shape=out_shapes,
            scratch_shapes=[pltpu.VMEM(s.shape, s.dtype) for s in scratch] + [pltpu.SemaphoreType.DMA((max(24, half + 4),))],
            compiler_params=pltpu.CompilerParams(vmem_limit_bytes=limit),
            cost_estimate=pl.CostEstimate(flops=flops, bytes_accessed=10**6, transcendentals=0),
            name=name,
        )(*args)

    def exchange(value, groups=None):
        return lax.all_to_all(value, "space", 0, 0, tiled=True, axis_index_groups=groups)

    local_flops = 2 * offsets * rows * channels * (rows + channels)
    shown, payload = call(
        publish_kernel, "publish", (features, border, wanted), [shown_like, array((half, 2, *shown_like.shape), BF16)],
        [block, border, wanted, array((TILE, channels), F32), shown_like], 10**8,
    )
    across = lax.ppermute(shown, "space", [(place, (place + half) % peers) for place in range(peers)])
    payload = lax.dynamic_update_slice(
        payload, jnp.broadcast_to(across, (half, 1, *across.shape)), (0, 1, 0, 0)
    ).reshape(published, channels)
    payload, other = lax.optimization_barrier((payload, other))
    received = exchange(payload, [list(range(half)), list(range(half, peers))])
    total, halo_onehot, places, columns = call(
        functools.partial(first_local_kernel, borders), "first_local", (features, codes, wanted, own, other),
        [total_like, onehot_like, places_like, columns_like],
        [block, codes, wanted, weights_like, picked_like, total_like, onehot_like, places_like, columns_like], local_flops,
    )
    latent, normed, send = call(
        encode_kernel, "encode",
        (features, total, received, halo_onehot, places, border, conv_bias, own, other), [block, block, sent_like],
        [block, total_like, published_like, onehot_like, places_like, border, conv_bias, weights_like, spread_like,
         block, block, sent_like], 10**9,
    )
    received = exchange(send)
    total, = call(
        second_local_kernel, "second_local", (normed, columns, own, other), [array((max(rows, PADDED_ROWS), channels), F32)],
        [block, columns_like, weights_like, picked_like, total_like], local_flops,
    )
    kept, passed = call(
        functools.partial(decode_kernel, cap), "decode",
        (latent, total, received, halo_onehot, conv_bias, own, other), [array((2, rows, channels), BF16), block],
        [block, total_like, sent_like, onehot_like, conv_bias, weights_like, spread_like, block], 10**9, DECODE_BYTES,
    )
    got = lax.ppermute(passed, "phase", swap)
    return lax.dynamic_update_slice(kept, got[None], (1 - phase, 0, 0))[None]


def solution(mesh):
    return jax.shard_map(
        body,
        mesh=mesh,
        in_specs=(
            P(None, "space", None),
            P("phase", None, None, None),
            P(),
            P("space", None),
            P("space", None),
            P("space", None, None),
        ),
        out_specs=P("phase", None, "space", None),
        check_vma=False,
    )
```

```python
import functools

import jax
import jax.numpy as jnp
from jax import lax
from jax.experimental import pallas as pl
from jax.experimental.pallas import tpu as pltpu
from jax.sharding import PartitionSpec as P

BF16 = jnp.bfloat16
F32 = jnp.float32
I32 = jnp.int32
TILE = 8
BLOCK = 128
VMEM_BYTES = 60 * 2**20
DECODE_BYTES = 50 * 2**20
PADDED_ROWS = 15 * 1024


def iota(shape, dim):
    return lax.broadcasted_iota(I32, shape, dim)


def onehot(column, width):
    return (column == iota((column.shape[0], width), 1)).astype(BF16)


def dot(a, b):
    return jnp.dot(a, b, preferred_element_type=F32)


def normalise(values):
    mean_square = jnp.mean(values * values, axis=1, keepdims=True)
    return (values * lax.rsqrt(mean_square + 1e-06)).astype(BF16)


def packing(slots, offsets):
    pack = 128 // slots if slots < 128 else 1
    return pack, -(-offsets // pack)


def lookup(column, row):
    shape = (column.shape[0], row.shape[1])
    named = jnp.where(column == iota(shape, 1), jnp.broadcast_to(row.astype(F32), shape), 0.0)
    return jnp.sum(named, axis=1, keepdims=True).astype(I32)


class Copies:
    def __init__(self, sems):
        self.sems = sems
        self.used = 0

    def start(self, source, target):
        copy = pltpu.make_async_copy(source, target, self.sems.at[self.used])
        self.used += 1
        copy.start()
        return copy

    def start_either(self, chosen, copy, other):
        sem = self.sems.at[self.used]
        self.used += 1
        copy, other = (pltpu.make_async_copy(source, target, sem) for source, target in (copy, other))
        pl.when(chosen)(copy.start)
        pl.when(jnp.logical_not(chosen))(other.start)
        return copy


def publish_kernel(
    features_ref, border_ref, wanted_ref, shown_ref, payload_ref, block_ref, border_v, wanted_v, aux_ref, shown_v, sems
):
    copies = Copies(sems)
    loads = [
        copies.start(features_ref.at[lax.axis_index("phase")], block_ref),
        copies.start(border_ref, border_v),
        copies.start(wanted_ref, wanted_v),
    ]
    for load in loads:
        load.wait()
    cap, peers = wanted_v.shape
    place = lookup(iota((border_v.shape[1], 1), 0), border_v[...])
    picked = dot(onehot(place, block_ref.shape[0]), block_ref[...])
    aux_ref[...] = jnp.zeros_like(aux_ref)
    aux_ref[0:cap, 0:peers] = wanted_v[...].astype(F32)
    shown_v[...] = jnp.concatenate([normalise(picked).astype(F32), aux_ref[...]], axis=0).astype(BF16)
    stores = [copies.start(shown_v, shown_ref)]
    for member in range(payload_ref.shape[0]):
        stores.append(copies.start(shown_v, payload_ref.at[member, 0]))
    for store in stores:
        store.wait()


def gather(codes, normed, picked_v, beside=lambda k: None):
    rows, channels = normed.shape
    offsets = codes.shape[1]
    for k in range(offsets):
        if k == offsets // 2:
            picked_v[:, k * channels : (k + 1) * channels] = normed
        else:
            picked_v[:, k * channels : (k + 1) * channels] = dot(onehot(codes[:, k : k + 1], rows), normed).astype(BF16)
        beside(k)


def convolved_blocks(picked_v, held_ref):
    rows = picked_v.shape[0]
    matrix = held_ref[...].reshape(picked_v.shape[1], held_ref.shape[2])
    for first in range(0, rows, BLOCK):
        span = pl.ds(first, BLOCK)
        yield span, dot(picked_v[span, :], matrix)


def slot_numbers(rows, per_peer, cap):
    row = iota((rows, 1), 0)
    peer = lax.div(row, per_peer)
    return peer, lax.rem(row - peer * per_peer, cap)


def halo_onehot_group(codes, slots, group, halo_onehot_v):
    rows, offsets = codes.shape
    pack, groups = packing(slots, offsets)
    width = slots * pack
    lane = iota((rows, width), 1)
    named = None
    for j in range(pack):
        k = group * pack + j
        code = codes[:, k : k + 1] + (j * slots - rows) if k < offsets else jnp.full((rows, 1), -1, I32)
        code = jnp.broadcast_to(code, (rows, width))
        named = code if named is None else jnp.where(lane >= j * slots, code, named)
    halo_onehot_v[:, group * width : (group + 1) * width] = (named == lane).astype(BF16)


def published_places(wanted, borders):
    cap, peers = wanted.shape
    half = peers // 2
    upper_here = (lax.axis_index("space") >= half).astype(I32)

    def block_start(peer):
        upper = (peer >= half).astype(I32)
        across = (upper != upper_here).astype(I32)
        return ((peer - half * upper) * 2 + across) * (borders + TILE)

    peer, slot = slot_numbers(peers * cap, cap, cap)
    mine = lax.dot_general(
        onehot(peer, peers), wanted.astype(BF16), (((1,), (1,)), ((), ())), preferred_element_type=F32
    )
    mine = jnp.sum(jnp.where(iota(mine.shape, 1) == slot, mine, 0.0), axis=1, keepdims=True).astype(I32)
    asker, place = slot_numbers(peers * TILE, TILE, cap)
    return jnp.concatenate([block_start(peer) + mine, block_start(asker) + borders + place], axis=0)


def first_local_kernel(
    borders, features_ref, codes_ref, wanted_ref, own_ref, other_ref,
    total_ref, halo_onehot_ref, places_ref, columns_ref,
    block_ref, codes_v, wanted_v, held_ref, picked_v, total_v, halo_onehot_v, places_v, columns_v, sems,
):
    phase = lax.axis_index("phase")
    copies = Copies(sems)
    loads = [
        copies.start(codes_ref, codes_v),
        copies.start(features_ref.at[phase], block_ref),
        copies.start(wanted_ref, wanted_v),
    ]
    weights_load = copies.start_either(phase == 0, (own_ref, held_ref), (other_ref, held_ref))
    for load in loads:
        load.wait()
    codes = codes_v[...].T
    columns_v[:, 0 : codes.shape[1]] = codes
    cap, peers = wanted_v.shape
    slots = peers * cap
    pack, groups = packing(slots, codes.shape[1])
    places_v[...] = jnp.broadcast_to(published_places(wanted_v[...], borders), places_v.shape)

    def beside(k):
        if k % pack == 0:
            halo_onehot_group(codes, slots, k // pack, halo_onehot_v)

    gather(codes, normalise(block_ref[...].astype(F32)), picked_v, beside)
    stores = [copies.start(places_v, places_ref), copies.start(columns_v, columns_ref), copies.start(halo_onehot_v, halo_onehot_ref)]
    weights_load.wait()
    for span, term in convolved_blocks(picked_v, held_ref):
        total_v[span, :] = term
        stores.append(copies.start(total_v.at[span], total_ref.at[span]))
    for store in stores:
        store.wait()


def pick_rows(places, source_ref):
    rows = source_ref.shape[0]
    step = next(n for n in range(min(rows, 1536) // 16 * 16, 0, -16) if rows % n == 0)
    found = None
    for first in range(0, rows, step):
        term = dot(onehot(places - first, step), source_ref[first : first + step, :])
        found = term if found is None else found + term
    return found


def spread_halo(halo, held_ref, spread_ref):
    slots, channels = halo.shape
    offsets = held_ref.shape[0]
    whole = spread_ref.shape[0]
    if whole > offsets * slots:
        spread_ref[offsets * slots : whole, :] = jnp.zeros((whole - offsets * slots, channels), BF16)
    for k in range(offsets):
        spread_ref[k * slots : (k + 1) * slots, :] = dot(halo, held_ref[k]).astype(BF16)


def halo_term(halo_onehot_v, span, spread_ref):
    total = None
    for first in range(0, spread_ref.shape[0], 2048):
        lanes = pl.ds(first, min(2048, spread_ref.shape[0] - first))
        term = dot(halo_onehot_v[span, lanes], spread_ref[lanes, :])
        total = term if total is None else total + term
    return total


def residual(values, convolved):
    return (values + jax.nn.silu(convolved)).astype(BF16)


def encode_kernel(
    features_ref, total_ref, received_ref, halo_onehot_ref, places_ref, border_ref, bias_ref, own_ref, other_ref,
    latent_ref, normed_ref, send_ref,
    block_ref, total_v, received_v, halo_onehot_v, places_v, border_v, bias_v, held_ref, spread_ref,
    latent_v, normed_v, send_v, sems,
):
    phase = lax.axis_index("phase")
    copies = Copies(sems)
    early = [
        copies.start(received_ref, received_v),
        copies.start(places_ref, places_v),
        copies.start(border_ref, border_v),
    ]
    weights_load = copies.start_either(phase == 0, (own_ref, held_ref), (other_ref, held_ref))
    late = [
        copies.start(halo_onehot_ref, halo_onehot_v),
        copies.start(total_ref, total_v),
        copies.start(features_ref.at[phase], block_ref),
        copies.start(bias_ref, bias_v),
    ]
    for load in early:
        load.wait()
    slots = places_v.shape[0] - send_v.shape[0]
    found = pick_rows(places_v[:, 0:1], received_v)
    theirs = jnp.where(iota((send_v.shape[0], found.shape[1]), 1) == lax.axis_index("space"), found[slots:], 0.0)
    asked = lookup(jnp.sum(theirs, axis=1, keepdims=True).astype(I32), border_v[...])
    weights_load.wait()
    spread_halo(found[:slots].astype(BF16), held_ref, spread_ref)
    for load in late:
        load.wait()
    term = halo_term(halo_onehot_v, pl.ds(0, block_ref.shape[0]), spread_ref)
    latent = residual(block_ref[...].astype(F32), total_v[...] + term + bias_v[0:1, :])
    latent_v[...] = latent
    stores = [copies.start(latent_v, latent_ref)]
    normed = normalise(latent.astype(F32))
    normed_v[...] = normed
    stores.append(copies.start(normed_v, normed_ref))
    out = dot(onehot(asked, normed.shape[0]), normed)
    width = send_v.shape[1]
    part = lax.rem(iota((send_v.shape[0], 1), 0), TILE)
    send_v[...] = jnp.where(part < TILE // 2, out[:, :width], out[:, width:]).astype(BF16)
    stores.append(copies.start(send_v, send_ref))
    for store in stores:
        store.wait()


def second_local_kernel(
    normed_ref, codes_ref, own_ref, other_ref, total_ref, normed_v, codes_v, held_ref, picked_v, total_v, sems
):
    phase = lax.axis_index("phase")
    copies = Copies(sems)
    early = [copies.start(codes_ref, codes_v), copies.start(normed_ref, normed_v)]
    weights_load = copies.start_either(phase == 1, (own_ref, held_ref), (other_ref, held_ref))
    for load in early:
        load.wait()
    gather(codes_v[:, 0 : picked_v.shape[1] // normed_v.shape[1]], normed_v[...], picked_v)
    weights_load.wait()
    stores = []
    for span, term in convolved_blocks(picked_v, held_ref):
        total_v[span, :] = term
        stores.append(copies.start(total_v.at[span], total_ref.at[span]))
    for store in stores:
        store.wait()


def decode_kernel(
    cap, latent_ref, total_ref, received_ref, halo_onehot_ref, bias_ref, own_ref, other_ref, kept_ref, passed_ref,
    latent_v, total_v, received_v, halo_onehot_v, bias_v, held_ref, spread_ref, recon_v, sems,
):
    first = lax.axis_index("phase") == 0
    copies = Copies(sems)
    received_load = copies.start(received_ref, received_v)
    weights_load = copies.start_either(first, (other_ref, held_ref), (own_ref, held_ref))
    late = [
        copies.start(halo_onehot_ref, halo_onehot_v),
        copies.start(total_ref.at[pl.ds(0, total_v.shape[0])], total_v),
        copies.start(latent_ref, latent_v),
        copies.start(bias_ref, bias_v),
    ]
    received_load.wait()
    peer, slot = slot_numbers(received_v.shape[0] // TILE * cap, cap, cap)
    halves = [pick_rows(peer * TILE + slot + cap * side, received_v).astype(BF16) for side in range(2)]
    halo = jnp.concatenate(halves, axis=1)
    weights_load.wait()
    spread_halo(halo, held_ref, spread_ref)
    for load in late:
        load.wait()
    stores = [copies.start_either(first, (latent_v, kept_ref.at[0]), (latent_v, passed_ref))]
    term = halo_term(halo_onehot_v, pl.ds(0, latent_v.shape[0]), spread_ref)
    recon_v[...] = residual(latent_v[...].astype(F32), total_v[...] + term + bias_v[1:2, :])
    stores.append(copies.start_either(first, (recon_v, passed_ref), (recon_v, kept_ref.at[1])))
    for store in stores:
        store.wait()


def body(features, weights, conv_bias, rulebook, border, pull_slots):
    micro, rows, channels = features.shape
    peers, cap = pull_slots.shape[1:]
    borders = border.shape[1]
    offsets = rulebook.shape[1]
    slots = peers * cap
    half = peers // 2
    pack, groups = packing(slots, offsets)
    published = peers * (borders + TILE)
    phase = lax.axis_index("phase")
    wanted = pull_slots[0].T
    codes = rulebook.T
    own = weights[0]
    swap = [(0, 1), (1, 0)]
    other = lax.ppermute(own, "phase", swap)

    anywhere = pl.BlockSpec(memory_space=pl.ANY)
    array = jax.ShapeDtypeStruct
    block = array((rows, channels), BF16)
    total_like = array((rows, channels), F32)
    published_like = array((published, channels), BF16)
    shown_like = array((borders + TILE, channels), BF16)
    sent_like = array((peers * TILE, channels // 2), BF16)
    onehot_like = array((rows, groups * pack * slots), BF16)
    places_like = array((slots + peers * TILE, 128), I32)
    columns_like = array((rows, -(-offsets // 128) * 128), I32)
    weights_like = array(own.shape, BF16)
    picked_like = array((rows, offsets * channels), BF16)
    spread_like = array((groups * pack * slots, channels), BF16)

    def call(kernel, name, args, out_shapes, scratch, flops, limit=VMEM_BYTES):
        return pl.pallas_call(
            kernel,
            in_specs=[anywhere] * len(args),
            out_specs=[anywhere] * len(out_shapes),
            out_shape=out_shapes,
            scratch_shapes=[pltpu.VMEM(s.shape, s.dtype) for s in scratch] + [pltpu.SemaphoreType.DMA((max(12, half + 4),))],
            compiler_params=pltpu.CompilerParams(vmem_limit_bytes=limit),
            cost_estimate=pl.CostEstimate(flops=flops, bytes_accessed=10**6, transcendentals=0),
            name=name,
        )(*args)

    def exchange(value, groups=None):
        return lax.all_to_all(value, "space", 0, 0, tiled=True, axis_index_groups=groups)

    local_flops = 2 * offsets * rows * channels * (rows + channels)
    shown, payload = call(
        publish_kernel, "publish", (features, border, wanted), [shown_like, array((half, 2, *shown_like.shape), BF16)],
        [block, border, wanted, array((TILE, channels), F32), shown_like], 10**8,
    )
    across = lax.ppermute(shown, "space", [(place, (place + half) % peers) for place in range(peers)])
    payload = lax.dynamic_update_slice(
        payload, jnp.broadcast_to(across, (half, 1, *across.shape)), (0, 1, 0, 0)
    ).reshape(published, channels)
    payload, other = lax.optimization_barrier((payload, other))
    received = exchange(payload, [list(range(half)), list(range(half, peers))])
    total, halo_onehot, places, columns = call(
        functools.partial(first_local_kernel, borders), "first_local", (features, codes, wanted, own, other),
        [total_like, onehot_like, places_like, columns_like],
        [block, codes, wanted, weights_like, picked_like, total_like, onehot_like, places_like, columns_like], local_flops,
    )
    latent, normed, send = call(
        encode_kernel, "encode",
        (features, total, received, halo_onehot, places, border, conv_bias, own, other), [block, block, sent_like],
        [block, total_like, published_like, onehot_like, places_like, border, conv_bias, weights_like, spread_like,
         block, block, sent_like], 10**9,
    )
    received = exchange(send)
    total, = call(
        second_local_kernel, "second_local", (normed, columns, own, other), [array((max(rows, PADDED_ROWS), channels), F32)],
        [block, columns_like, weights_like, picked_like, total_like], local_flops,
    )
    kept, passed = call(
        functools.partial(decode_kernel, cap), "decode",
        (latent, total, received, halo_onehot, conv_bias, own, other), [array((2, rows, channels), BF16), block],
        [block, total_like, sent_like, onehot_like, conv_bias, weights_like, spread_like, block], 10**9, DECODE_BYTES,
    )
    got = lax.ppermute(passed, "phase", swap)
    return lax.dynamic_update_slice(kept, got[None], (1 - phase, 0, 0))[None]


def solution(mesh):
    return jax.shard_map(
        body,
        mesh=mesh,
        in_specs=(
            P(None, "space", None),
            P("phase", None, None, None),
            P(),
            P("space", None),
            P("space", None),
            P("space", None, None),
        ),
        out_specs=P("phase", None, "space", None),
        check_vma=False,
    )
```

```python
import functools

import jax
import jax.numpy as jnp
from jax import lax
from jax.experimental import pallas as pl
from jax.experimental.pallas import tpu as pltpu
from jax.sharding import PartitionSpec as P

BF16 = jnp.bfloat16
F32 = jnp.float32
I32 = jnp.int32
TILE = 8
BLOCK = 128
VMEM_BYTES = 60 * 2**20
DECODE_BYTES = 50 * 2**20
PADDED_ROWS = 15 * 1024


def iota(shape, dim):
    return lax.broadcasted_iota(I32, shape, dim)


def onehot(column, width):
    return (column == iota((column.shape[0], width), 1)).astype(BF16)


def dot(a, b):
    return jnp.dot(a, b, preferred_element_type=F32)


def normalise(values):
    mean_square = jnp.mean(values * values, axis=1, keepdims=True)
    return (values * lax.rsqrt(mean_square + 1e-06)).astype(BF16)


def packing(slots, offsets):
    pack = 128 // slots if slots < 128 else 1
    return pack, -(-offsets // pack)


def lookup(column, row):
    shape = (column.shape[0], row.shape[1])
    named = jnp.where(column == iota(shape, 1), jnp.broadcast_to(row.astype(F32), shape), 0.0)
    return jnp.sum(named, axis=1, keepdims=True).astype(I32)


class Copies:
    def __init__(self, sems):
        self.sems = sems
        self.used = 0

    def start(self, source, target):
        copy = pltpu.make_async_copy(source, target, self.sems.at[self.used])
        self.used += 1
        copy.start()
        return copy

    def start_either(self, chosen, copy, other):
        sem = self.sems.at[self.used]
        self.used += 1
        copy, other = (pltpu.make_async_copy(source, target, sem) for source, target in (copy, other))
        pl.when(chosen)(copy.start)
        pl.when(jnp.logical_not(chosen))(other.start)
        return copy


def publish_kernel(
    features_ref, border_ref, wanted_ref, shown_ref, payload_ref, block_ref, border_v, wanted_v, aux_ref, shown_v, sems
):
    copies = Copies(sems)
    loads = [
        copies.start(features_ref.at[lax.axis_index("phase")], block_ref),
        copies.start(border_ref, border_v),
        copies.start(wanted_ref, wanted_v),
    ]
    for load in loads:
        load.wait()
    cap, peers = wanted_v.shape
    place = lookup(iota((border_v.shape[1], 1), 0), border_v[...])
    picked = dot(onehot(place, block_ref.shape[0]), block_ref[...])
    aux_ref[...] = jnp.zeros_like(aux_ref)
    aux_ref[0:cap, 0:peers] = wanted_v[...].astype(F32)
    shown_v[...] = jnp.concatenate([normalise(picked).astype(F32), aux_ref[...]], axis=0).astype(BF16)
    stores = [copies.start(shown_v, shown_ref)]
    for member in range(payload_ref.shape[0]):
        stores.append(copies.start(shown_v, payload_ref.at[member, 0]))
    for store in stores:
        store.wait()


def gather(codes, normed, picked_v, beside=lambda k: None):
    rows, channels = normed.shape
    offsets = codes.shape[1]
    for k in range(offsets):
        if k == offsets // 2:
            picked_v[:, k * channels : (k + 1) * channels] = normed
        else:
            picked_v[:, k * channels : (k + 1) * channels] = dot(onehot(codes[:, k : k + 1], rows), normed).astype(BF16)
        beside(k)


def convolved_blocks(picked_v, held_ref):
    rows = picked_v.shape[0]
    matrix = held_ref[...].reshape(picked_v.shape[1], held_ref.shape[2])
    for first in range(0, rows, BLOCK):
        span = pl.ds(first, BLOCK)
        yield span, dot(picked_v[span, :], matrix)


def slot_numbers(rows, per_peer, cap):
    row = iota((rows, 1), 0)
    peer = lax.div(row, per_peer)
    return peer, lax.rem(row - peer * per_peer, cap)


def halo_onehot_group(codes, slots, group, halo_onehot_v):
    rows, offsets = codes.shape
    pack, groups = packing(slots, offsets)
    width = slots * pack
    lane = iota((rows, width), 1)
    named = None
    for j in range(pack):
        k = group * pack + j
        code = codes[:, k : k + 1] + (j * slots - rows) if k < offsets else jnp.full((rows, 1), -1, I32)
        code = jnp.broadcast_to(code, (rows, width))
        named = code if named is None else jnp.where(lane >= j * slots, code, named)
    halo_onehot_v[:, group * width : (group + 1) * width] = (named == lane).astype(BF16)


def published_places(wanted, borders):
    cap, peers = wanted.shape
    half = peers // 2
    upper_here = (lax.axis_index("space") >= half).astype(I32)

    def block_start(peer):
        upper = (peer >= half).astype(I32)
        across = (upper != upper_here).astype(I32)
        return ((peer - half * upper) * 2 + across) * (borders + TILE)

    peer, slot = slot_numbers(peers * cap, cap, cap)
    mine = lax.dot_general(
        onehot(peer, peers), wanted.astype(BF16), (((1,), (1,)), ((), ())), preferred_element_type=F32
    )
    mine = jnp.sum(jnp.where(iota(mine.shape, 1) == slot, mine, 0.0), axis=1, keepdims=True).astype(I32)
    asker, place = slot_numbers(peers * TILE, TILE, cap)
    return jnp.concatenate([block_start(peer) + mine, block_start(asker) + borders + place], axis=0)


def first_local_kernel(
    borders, features_ref, codes_ref, wanted_ref, own_ref, other_ref,
    total_ref, halo_onehot_ref, places_ref, columns_ref,
    block_ref, codes_v, wanted_v, held_ref, picked_v, total_v, halo_onehot_v, places_v, columns_v, sems,
):
    phase = lax.axis_index("phase")
    copies = Copies(sems)
    loads = [
        copies.start(codes_ref, codes_v),
        copies.start(features_ref.at[phase], block_ref),
        copies.start(wanted_ref, wanted_v),
    ]
    weights_load = copies.start_either(phase == 0, (own_ref, held_ref), (other_ref, held_ref))
    for load in loads:
        load.wait()
    codes = codes_v[...].T
    columns_v[:, 0 : codes.shape[1]] = codes
    cap, peers = wanted_v.shape
    slots = peers * cap
    pack, groups = packing(slots, codes.shape[1])
    places_v[...] = jnp.broadcast_to(published_places(wanted_v[...], borders), places_v.shape)

    def beside(k):
        if k % pack == 0:
            halo_onehot_group(codes, slots, k // pack, halo_onehot_v)

    gather(codes, normalise(block_ref[...].astype(F32)), picked_v, beside)
    stores = [copies.start(places_v, places_ref), copies.start(columns_v, columns_ref), copies.start(halo_onehot_v, halo_onehot_ref)]
    weights_load.wait()
    for span, term in convolved_blocks(picked_v, held_ref):
        total_v[span, :] = term
        stores.append(copies.start(total_v.at[span], total_ref.at[span]))
    for store in stores:
        store.wait()


def pick_rows(places, source_ref):
    rows = source_ref.shape[0]
    step = next(n for n in range(min(rows, 1536) // 16 * 16, 0, -16) if rows % n == 0)
    found = None
    for first in range(0, rows, step):
        term = dot(onehot(places - first, step), source_ref[first : first + step, :])
        found = term if found is None else found + term
    return found


def spread_halo(halo, held_ref, spread_ref):
    slots, channels = halo.shape
    offsets = held_ref.shape[0]
    whole = spread_ref.shape[0]
    if whole > offsets * slots:
        spread_ref[offsets * slots : whole, :] = jnp.zeros((whole - offsets * slots, channels), BF16)
    for k in range(offsets):
        spread_ref[k * slots : (k + 1) * slots, :] = dot(halo, held_ref[k]).astype(BF16)


def halo_term(halo_onehot_v, span, spread_ref):
    total = None
    for first in range(0, spread_ref.shape[0], 2048):
        lanes = pl.ds(first, min(2048, spread_ref.shape[0] - first))
        term = dot(halo_onehot_v[span, lanes], spread_ref[lanes, :])
        total = term if total is None else total + term
    return total


def residual(values, convolved):
    return (values + jax.nn.silu(convolved)).astype(BF16)


def encode_kernel(
    features_ref, total_ref, received_ref, halo_onehot_ref, places_ref, border_ref, bias_ref, own_ref, other_ref,
    latent_ref, normed_ref, send_ref,
    block_ref, total_v, received_v, halo_onehot_v, places_v, border_v, bias_v, held_ref, spread_ref,
    latent_v, normed_v, send_v, sems,
):
    phase = lax.axis_index("phase")
    copies = Copies(sems)
    early = [
        copies.start(received_ref, received_v),
        copies.start(places_ref, places_v),
        copies.start(border_ref, border_v),
    ]
    weights_load = copies.start_either(phase == 0, (own_ref, held_ref), (other_ref, held_ref))
    late = [
        copies.start(halo_onehot_ref, halo_onehot_v),
        copies.start(total_ref, total_v),
        copies.start(features_ref.at[phase], block_ref),
        copies.start(bias_ref, bias_v),
    ]
    for load in early:
        load.wait()
    slots = places_v.shape[0] - send_v.shape[0]
    found = pick_rows(places_v[:, 0:1], received_v)
    theirs = jnp.where(iota((send_v.shape[0], found.shape[1]), 1) == lax.axis_index("space"), found[slots:], 0.0)
    asked = lookup(jnp.sum(theirs, axis=1, keepdims=True).astype(I32), border_v[...])
    weights_load.wait()
    spread_halo(found[:slots].astype(BF16), held_ref, spread_ref)
    for load in late:
        load.wait()
    term = halo_term(halo_onehot_v, pl.ds(0, block_ref.shape[0]), spread_ref)
    latent = residual(block_ref[...].astype(F32), total_v[...] + term + bias_v[0:1, :])
    latent_v[...] = latent
    normed = normalise(latent.astype(F32))
    normed_v[...] = normed
    out = dot(onehot(asked, normed.shape[0]), normed)
    width = send_v.shape[1]
    part = lax.rem(iota((send_v.shape[0], 1), 0), TILE)
    send_v[...] = jnp.where(part < TILE // 2, out[:, :width], out[:, width:]).astype(BF16)
    stores = [
        copies.start(send_v, send_ref),
        copies.start(normed_v, normed_ref),
        copies.start(latent_v, latent_ref),
    ]
    for store in stores:
        store.wait()


def second_local_kernel(
    normed_ref, codes_ref, own_ref, other_ref, total_ref, normed_v, codes_v, held_ref, picked_v, total_v, sems
):
    phase = lax.axis_index("phase")
    copies = Copies(sems)
    early = [copies.start(codes_ref, codes_v), copies.start(normed_ref, normed_v)]
    weights_load = copies.start_either(phase == 1, (own_ref, held_ref), (other_ref, held_ref))
    for load in early:
        load.wait()
    gather(codes_v[:, 0 : picked_v.shape[1] // normed_v.shape[1]], normed_v[...], picked_v)
    weights_load.wait()
    stores = []
    for span, term in convolved_blocks(picked_v, held_ref):
        total_v[span, :] = term
        stores.append(copies.start(total_v.at[span], total_ref.at[span]))
    for store in stores:
        store.wait()


def decode_kernel(
    cap, latent_ref, total_ref, received_ref, halo_onehot_ref, bias_ref, own_ref, other_ref, kept_ref, passed_ref,
    latent_v, total_v, received_v, halo_onehot_v, bias_v, held_ref, spread_ref, recon_v, sems,
):
    first = lax.axis_index("phase") == 0
    copies = Copies(sems)
    received_load = copies.start(received_ref, received_v)
    weights_load = copies.start_either(first, (other_ref, held_ref), (own_ref, held_ref))
    late = [
        copies.start(halo_onehot_ref, halo_onehot_v),
        copies.start(total_ref.at[pl.ds(0, total_v.shape[0])], total_v),
        copies.start(latent_ref, latent_v),
        copies.start(bias_ref, bias_v),
    ]
    received_load.wait()
    peer, slot = slot_numbers(received_v.shape[0] // TILE * cap, cap, cap)
    halves = [pick_rows(peer * TILE + slot + cap * side, received_v).astype(BF16) for side in range(2)]
    halo = jnp.concatenate(halves, axis=1)
    weights_load.wait()
    spread_halo(halo, held_ref, spread_ref)
    for load in late:
        load.wait()
    stores = [copies.start_either(first, (latent_v, kept_ref.at[0]), (latent_v, passed_ref))]
    term = halo_term(halo_onehot_v, pl.ds(0, latent_v.shape[0]), spread_ref)
    recon_v[...] = residual(latent_v[...].astype(F32), total_v[...] + term + bias_v[1:2, :])
    stores.append(copies.start_either(first, (recon_v, passed_ref), (recon_v, kept_ref.at[1])))
    for store in stores:
        store.wait()


def body(features, weights, conv_bias, rulebook, border, pull_slots):
    micro, rows, channels = features.shape
    peers, cap = pull_slots.shape[1:]
    borders = border.shape[1]
    offsets = rulebook.shape[1]
    slots = peers * cap
    half = peers // 2
    pack, groups = packing(slots, offsets)
    published = peers * (borders + TILE)
    phase = lax.axis_index("phase")
    wanted = pull_slots[0].T
    codes = rulebook.T
    own = weights[0]
    swap = [(0, 1), (1, 0)]
    other = lax.ppermute(own, "phase", swap)

    anywhere = pl.BlockSpec(memory_space=pl.ANY)
    array = jax.ShapeDtypeStruct
    block = array((rows, channels), BF16)
    total_like = array((rows, channels), F32)
    published_like = array((published, channels), BF16)
    shown_like = array((borders + TILE, channels), BF16)
    sent_like = array((peers * TILE, channels // 2), BF16)
    onehot_like = array((rows, groups * pack * slots), BF16)
    places_like = array((slots + peers * TILE, 128), I32)
    columns_like = array((rows, -(-offsets // 128) * 128), I32)
    weights_like = array(own.shape, BF16)
    picked_like = array((rows, offsets * channels), BF16)
    spread_like = array((groups * pack * slots, channels), BF16)

    def call(kernel, name, args, out_shapes, scratch, flops, limit=VMEM_BYTES):
        return pl.pallas_call(
            kernel,
            in_specs=[anywhere] * len(args),
            out_specs=[anywhere] * len(out_shapes),
            out_shape=out_shapes,
            scratch_shapes=[pltpu.VMEM(s.shape, s.dtype) for s in scratch] + [pltpu.SemaphoreType.DMA((max(12, half + 4),))],
            compiler_params=pltpu.CompilerParams(vmem_limit_bytes=limit),
            cost_estimate=pl.CostEstimate(flops=flops, bytes_accessed=10**6, transcendentals=0),
            name=name,
        )(*args)

    def exchange(value, groups=None):
        return lax.all_to_all(value, "space", 0, 0, tiled=True, axis_index_groups=groups)

    local_flops = 2 * offsets * rows * channels * (rows + channels)
    shown, payload = call(
        publish_kernel, "publish", (features, border, wanted), [shown_like, array((half, 2, *shown_like.shape), BF16)],
        [block, border, wanted, array((TILE, channels), F32), shown_like], 10**8,
    )
    across = lax.ppermute(shown, "space", [(place, (place + half) % peers) for place in range(peers)])
    payload = lax.dynamic_update_slice(
        payload, jnp.broadcast_to(across, (half, 1, *across.shape)), (0, 1, 0, 0)
    ).reshape(published, channels)
    payload, other = lax.optimization_barrier((payload, other))
    received = exchange(payload, [list(range(half)), list(range(half, peers))])
    total, halo_onehot, places, columns = call(
        functools.partial(first_local_kernel, borders), "first_local", (features, codes, wanted, own, other),
        [total_like, onehot_like, places_like, columns_like],
        [block, codes, wanted, weights_like, picked_like, total_like, onehot_like, places_like, columns_like], local_flops,
    )
    latent, normed, send = call(
        encode_kernel, "encode",
        (features, total, received, halo_onehot, places, border, conv_bias, own, other), [block, block, sent_like],
        [block, total_like, published_like, onehot_like, places_like, border, conv_bias, weights_like, spread_like,
         block, block, sent_like], 10**9,
    )
    received = exchange(send)
    total, = call(
        second_local_kernel, "second_local", (normed, columns, own, other), [array((max(rows, PADDED_ROWS), channels), F32)],
        [block, columns_like, weights_like, picked_like, total_like], local_flops,
    )
    kept, passed = call(
        functools.partial(decode_kernel, cap), "decode",
        (latent, total, received, halo_onehot, conv_bias, own, other), [array((2, rows, channels), BF16), block],
        [block, total_like, sent_like, onehot_like, conv_bias, weights_like, spread_like, block], 10**9, DECODE_BYTES,
    )
    got = lax.ppermute(passed, "phase", swap)
    return lax.dynamic_update_slice(kept, got[None], (1 - phase, 0, 0))[None]


def solution(mesh):
    return jax.shard_map(
        body,
        mesh=mesh,
        in_specs=(
            P(None, "space", None),
            P("phase", None, None, None),
            P(),
            P("space", None),
            P("space", None),
            P("space", None, None),
        ),
        out_specs=P("phase", None, "space", None),
        check_vma=False,
    )
```
